32 devices in a mesh: context: 8 (over y, x, core), tensor: 4 (over z).
Axes of the slice: x: 2, y: 2, z: 4, core: 2. Of those that a mesh axis runs over, the one named last changes fastest.
Arguments:
- projected: bfloat16 [3, 3072, 8192], P(None, 'context', 'tensor'), may hold values from -6 to 6
- taps: float32 [3, 3, 8192], P(None, None, 'tensor'), may hold values from -4 to 4
- filters: bfloat16 [512, 128], P('tensor'), may hold values from -0.5 to 0.5
- skip: float32 [8192], P('tensor'), may hold values from -4 to 4
- out_weight: bfloat16 [8192, 8192], P('tensor', 'context'), may hold values from -0.09375 to 0.09375
- positions: int32 [32], replicated, may hold values from 0 to 3071
Outputs:
- mixed: bfloat16 [3072, 8192], P('context', 'tensor')
- variant_states: bfloat16 [32, 8192], P('context', 'tensor')
The draws below stay inside these ranges and needn't reach their ends.
All inputs are finite; a program needn't handle non-finite values.
Results may differ from the reference program's by a relative error of at most 0.018.
Values may be sent and summed in bfloat16 or wider, within the bound.
A program may use at most 192 MiB of HBM per device.

```python
import jax
import jax.numpy as jnp
from jax import lax

D = 8192
FLT = 128
GROUP = 16
SHORT = 3
GROUPS = 512
TOKENS = 3072
VARIANTS = 32
N_TENSOR = 4


def touch_ends(entries, own_key, low, top_value):
    extent = entries.shape
    spot = [jax.random.randint(jax.random.fold_in(own_key, axis), (), 0, extent[axis]) for axis in range(len(extent))]
    entries = entries.at[tuple(spot)].set(low)
    longest = extent.index(max(extent))
    spot[longest] = (spot[longest] + 1) % extent[longest]
    return entries.at[tuple(spot)].set(top_value)


def raised(array, stream_key, source, target, blocks, factor):
    owner, partner = [(jnp.arange(array.shape[axis_at]) // (array.shape[axis_at] // blocks)).reshape([-1 if axis == axis_at else 1 for axis in range(array.ndim)]) for axis_at in (source, target)]
    chosen = jax.random.permutation(stream_key, blocks)[partner]
    strong = (owner == chosen) | (owner == (partner + blocks // 2) % blocks)
    return jnp.where(strong, factor * array, array)


def block_levels(key, shape, cuts, low, top_value):
    def one(axis_at, blocks):
        heights = jax.random.uniform(jax.random.fold_in(jax.random.fold_in(key, 6), axis_at), (blocks,), jnp.float32, low / len(cuts), top_value / len(cuts))
        return jnp.repeat(jnp.exp(heights), shape[axis_at] // blocks).reshape((-1,) + (1,) * (len(shape) - axis_at - 1))

    level = one(*cuts[0])
    for cut in cuts[1:]:
        level = level * one(*cut)
    return level


def gaussian(stream_key, dims, deviation, reach, cuts=(), dtype=jnp.bfloat16):
    entries = deviation * jax.random.normal(stream_key, dims, jnp.float32)
    if cuts:
        entries = entries * block_levels(stream_key, dims, cuts, -0.22, 0.18)
    return jnp.clip(entries, -reach, reach).astype(dtype)


def gaussian_with(key, dims, scale, most, cuts, heavy, held_as=jnp.bfloat16):
    array = scale * jax.random.normal(key, dims, jnp.float32)
    if cuts:
        array = array * block_levels(key, dims, cuts, -0.22, 0.18)
    return jnp.clip(raised(array, jax.random.fold_in(key, 3), *heavy), -most, most).astype(held_as)


def setup_inputs(seed: int = 0) -> dict:
    seeds = jax.random.split(jax.random.key(seed), 7)
    return {
        "projected": gaussian(seeds[0], (3, TOKENS, D), 1.0, 6.0, ((1, 8), (2, 4))),
        "taps": gaussian(seeds[1], (3, SHORT, D), 0.6, 4.0, ((2, 4),), jnp.float32),
        "filters": gaussian(seeds[2], (GROUPS, FLT), FLT ** -0.5, 0.5, ((0, 4),)),
        "skip": gaussian(seeds[3], (D,), 1.0, 4.0, ((0, 4),), jnp.float32),
        "out_weight": gaussian_with(seeds[4], (D, D), D ** -0.5, 0.09375, ((0, 4), (1, 8)), (0, 1, 8, 2.0)),
        "positions": touch_ends(jax.random.randint(seeds[5], (VARIANTS,), 0, TOKENS), jax.random.fold_in(seeds[5], 1), 0, TOKENS - 1).astype(jnp.int32),
    }


def reference(projected, taps, filters, skip, out_weight, positions):
    inputs = projected.astype(jnp.float32)
    padded = jnp.pad(inputs, ((0, 0), (SHORT - 1, 0), (0, 0)))
    feat = jnp.zeros_like(inputs)
    for lag in range(SHORT):
        feat = feat + taps[:, lag, None, :] * padded[:, SHORT - 1 - lag:SHORT - 1 - lag + TOKENS, :]
    query = feat[0]
    product = (feat[1] * feat[2]).astype(jnp.bfloat16)
    product_f = product.astype(jnp.float32)
    per_channel = jnp.repeat(filters.astype(jnp.float32), GROUP, axis=0)
    shifted = jnp.pad(product_f, ((FLT - 1, 0), (0, 0)))

    def add_tap(lag, total):
        window = lax.dynamic_slice_in_dim(shifted, FLT - 1 - lag, TOKENS, 0)
        column = lax.dynamic_slice_in_dim(per_channel, lag, 1, 1)[:, 0]
        return total + column[None, :] * window

    conv = lax.fori_loop(0, FLT, add_tap, skip[None, :] * product_f)
    gated = (query * conv).astype(jnp.bfloat16)
    width = D // N_TENSOR
    mixed = jnp.zeros((TOKENS, D), jnp.float32)
    for block in range(N_TENSOR):
        part = jnp.dot(gated[:, block * width:(block + 1) * width], out_weight[block * width:(block + 1) * width, :], preferred_element_type=jnp.float32)
        mixed = mixed + part.astype(jnp.bfloat16).astype(jnp.float32)
    mixed_out = mixed.astype(jnp.bfloat16)
    variant_states = jnp.take(mixed_out, positions, axis=0)
    return mixed_out, variant_states
```

```python
import jax
import jax.numpy as jnp
from jax import lax
from jax.experimental import pallas as pl
from jax.experimental.pallas import tpu as pltpu
from jax.sharding import PartitionSpec as P

FLT = 128
GROUP = 16
SHORT = 3


def shifted(array, axis, by):
    size = lax.axis_size(axis)
    pairs = [(i, i + by) for i in range(size) if 0 <= i + by < size]
    return lax.ppermute(array, axis, pairs)


def short_filter(extended, weights, count):
    lags = SHORT - 1
    total = jnp.zeros((extended.shape[0], count, extended.shape[2]), jnp.float32)
    for lag in range(SHORT):
        total = total + weights[:, lag, None, :] * extended[
            :, lags - lag : lags - lag + count, :
        ].astype(jnp.float32)
    return total


def banded_filters(filters, rows):
    local_groups = filters.shape[0]
    span = FLT - 1 + rows
    reversed_taps = jnp.flip(filters, axis=1)
    padded_taps = jnp.concatenate(
        [reversed_taps, jnp.zeros((local_groups, rows), filters.dtype)], axis=1
    )
    tiled = jnp.tile(padded_taps, (1, rows))
    return tiled[:, : rows * span].reshape(local_groups, rows, span)


def on_device(projected, taps, filters, skip, out_weight, positions):
    rows = projected.shape[1]
    width = projected.shape[2]
    lags = SHORT - 1
    reach = FLT - 1
    rim = shifted(projected[:, rows - lags :, :], "context", 1)
    feat = short_filter(jnp.concatenate([rim, projected], axis=1), taps, rows)
    query = feat[0]
    product = (feat[1] * feat[2]).astype(jnp.bfloat16)
    prior = shifted(product[rows - reach :], "context", 1)
    extended = jnp.concatenate([prior, product], axis=0)
    span = reach + rows
    toeplitz = banded_filters(filters, rows)
    local_groups = filters.shape[0]
    conv = jnp.einsum(
        "gim,mgc->igc",
        toeplitz,
        extended.reshape(span, local_groups, GROUP),
        preferred_element_type=jnp.float32,
    ).reshape(rows, width)
    conv = conv + skip[None, :] * product.astype(jnp.float32)
    gated = (query * conv).astype(jnp.bfloat16)
    terms = jnp.dot(
        gated,
        lax.all_gather(out_weight, "context", axis=1, tiled=True),
        preferred_element_type=jnp.float32,
    )
    mixed = lax.psum_scatter(terms.astype(jnp.bfloat16), "tensor", scatter_dimension=1, tiled=True)
    offset = lax.axis_index("context") * rows
    local_sites = positions - offset
    one_hot = (local_sites[:, None] == jnp.arange(rows, dtype=jnp.int32)[None, :]).astype(
        jnp.bfloat16
    )
    picked_terms = jnp.dot(one_hot, mixed, preferred_element_type=jnp.float32)
    variant_states = lax.psum_scatter(
        picked_terms.astype(jnp.bfloat16), "context", scatter_dimension=0, tiled=True
    )
    return (mixed, variant_states)


LANES = 128
PIECES = 4
LAG = 2
HALO = 144
RIM = 16
SLOTS = 16
MESH = pl.DeviceIdType.MESH


def flip(index, bit):
    return index + bit - 2 * bit * ((index // bit) % 2)


def arrival(step):
    later = step - 8
    slot = later // 4
    way = later % 4
    part = slot // 2
    side = slot % 2
    via_y = way % 2
    mid = jnp.where(part == 1, 1, 0)
    first = jnp.where(part == 0, 1, 0)
    owner_x = 2 + 4 * mid
    piece_x = side + 2 * (1 - first)
    owner_y = 4 + 2 * mid
    piece_y = side + 2 * first
    owner = jnp.where(via_y == 1, owner_y, owner_x) + way // 2
    piece = jnp.where(via_y == 1, piece_y, piece_x)
    own = step < 8
    return jnp.where(own, step // 4, owner), jnp.where(own, step % 4, piece)


def fused(
    proj, taps, bands, skip, weight, sites, mixed, picked,
    ext, held, gated, stage, main, extra, outbox, inbox,
    local_sem, halo_send, halo_recv, x_send, y_send, core_send, held_recv,
    z_send, main_recv, extra_recv, pick_send, pick_recv,
):
    rows, width = gated.shape
    cols = held.shape[2]
    c = lax.axis_index("context")
    z = lax.axis_index("tensor")
    n_context = lax.axis_size("context")
    n_tensor = lax.axis_size("tensor")
    to_x, to_y, to_core = flip(c, 2), flip(c, 4), flip(c, 1)

    barrier = pltpu.get_barrier_semaphore()
    for step in range(1, n_context):
        pl.semaphore_signal(
            barrier, inc=1, device_id={"context": lax.rem(c + step, n_context)}, device_id_type=MESH
        )

    @pl.when(z > 0)
    def _():
        pl.semaphore_signal(barrier, inc=1, device_id={"tensor": z - 1}, device_id_type=MESH)

    @pl.when(z < n_tensor - 1)
    def _():
        pl.semaphore_signal(barrier, inc=1, device_id={"tensor": z + 1}, device_id_type=MESH)

    own_copies = [
        pltpu.make_async_copy(
            weight.at[:, pl.ds(piece * cols, cols)], held.at[piece], local_sem.at[piece]
        )
        for piece in range(PIECES)
    ]
    for copy in own_copies:
        copy.start()
    load = pltpu.make_async_copy(proj, ext.at[:, pl.ds(HALO, rows), :], local_sem.at[PIECES])
    load.start()

    inner = jnp.logical_and(z > 0, z < n_tensor - 1)
    pl.semaphore_wait(barrier, n_context + jnp.where(inner, 1, 0))

    def halo_copies(target):
        return (
            pltpu.make_async_remote_copy(
                src_ref=proj.at[pl.ds(1, 2), pl.ds(rows - HALO, HALO), :],
                dst_ref=ext.at[pl.ds(1, 2), pl.ds(0, HALO), :],
                send_sem=halo_send.at[0], recv_sem=halo_recv.at[0],
                device_id={"context": target}, device_id_type=MESH,
            ),
            pltpu.make_async_remote_copy(
                src_ref=proj.at[0, pl.ds(rows - RIM, RIM), :],
                dst_ref=ext.at[0, pl.ds(HALO - RIM, RIM), :],
                send_sem=halo_send.at[1], recv_sem=halo_recv.at[1],
                device_id={"context": target}, device_id_type=MESH,
            ),
        )

    @pl.when(c < n_context - 1)
    def _():
        for copy in halo_copies(c + 1):
            copy.start()

    def send_held(source, landing, send_sem, target):
        return pltpu.make_async_remote_copy(
            src_ref=held.at[source], dst_ref=held.at[landing],
            send_sem=send_sem, recv_sem=held_recv.at[landing],
            device_id={"context": target}, device_id_type=MESH,
        )

    for copy in own_copies:
        copy.wait()
    for piece in (0, 1):
        send_held(piece, 2 * PIECES + piece, x_send.at[piece], to_x).start()
        send_held(piece + 2, 4 * PIECES + piece + 2, y_send.at[piece + 2], to_y).start()
    for piece in range(PIECES):
        send_held(piece, PIECES + piece, core_send.at[piece], to_core).start()

    load.wait()

    @pl.when(c == 0)
    def _():
        ext[:, pl.ds(0, HALO), :] = jnp.zeros((3, HALO, width), ext.dtype)

    @pl.when(c > 0)
    def _():
        for copy in halo_copies(c):
            copy.wait_recv()

    blocks = rows // FLT
    per_tile = LANES // GROUP

    @pl.loop(0, width // LANES)
    def _(tile):
        lanes = pl.ds(pl.multiple_of(tile * LANES, LANES), LANES)

        def feature(which, start):
            values = ext[which, pl.ds(start - RIM, HALO + rows - start + RIM), lanes].astype(jnp.float32)
            count = values.shape[0] - RIM
            weights = taps[which, :, lanes]
            total = weights[0:1] * values[RIM:]
            for lag in range(1, SHORT):
                total = total + weights[lag : lag + 1] * values[RIM - lag : RIM - lag + count]
            return total

        query = feature(0, HALO)
        product = (feature(1, RIM) * feature(2, RIM)).astype(jnp.bfloat16)
        wide = jnp.concatenate(
            [product[b * FLT : (b + 2) * FLT] for b in range(blocks)], axis=1
        )
        group_of = lax.broadcasted_iota(jnp.int32, (FLT, blocks * LANES), 1) % LANES // GROUP
        total = jnp.zeros((FLT, blocks * LANES), jnp.float32)
        for g in range(per_tile):
            row = bands[pl.ds(tile * per_tile + g, 1), :]
            band = pltpu.roll(
                jnp.broadcast_to(row, (FLT, 2 * FLT)), 0, 1, stride=1, stride_axis=0
            ).astype(jnp.bfloat16)
            term = jnp.dot(band, wide, preferred_element_type=jnp.float32)
            total = jnp.where(group_of == g, term, total)
        direct = skip[:, lanes]
        for b in range(blocks):
            here = product[(b + 1) * FLT : (b + 2) * FLT].astype(jnp.float32)
            conv = total[:, b * LANES : (b + 1) * LANES] + direct * here
            gated[pl.ds(b * FLT, FLT), lanes] = (
                query[b * FLT : (b + 1) * FLT] * conv
            ).astype(jnp.bfloat16)

    def place(owner, piece):
        up_y = (c // 4 + owner // 4) % 2
        up_x = (c // 2 + owner // 2) % 2
        up_core = (c + owner) % 2
        return owner * PIECES + piece, 2 * up_y + up_x, up_core * PIECES + piece

    def up_copy(slot):
        return pltpu.make_async_remote_copy(
            src_ref=stage.at[slot], dst_ref=main.at[slot],
            send_sem=z_send.at[slot], recv_sem=main_recv.at[slot],
            device_id={"tensor": z + 1}, device_id_type=MESH,
        )

    def down_copy(slot):
        return pltpu.make_async_remote_copy(
            src_ref=stage.at[slot], dst_ref=main.at[slot],
            send_sem=z_send.at[slot], recv_sem=main_recv.at[slot],
            device_id={"tensor": z - 1}, device_id_type=MESH,
        )

    def last_copy(slot, block):
        return pltpu.make_async_remote_copy(
            src_ref=stage.at[slot], dst_ref=extra.at[block],
            send_sem=z_send.at[slot], recv_sem=extra_recv.at[block],
            device_id={"tensor": z - 1}, device_id_type=MESH,
        )

    def pass_on(slot, goal, block):
        @pl.when(goal > z)
        def _():
            up_copy(slot).start()

        @pl.when(goal < z - 1)
        def _():
            down_copy(slot).start()

        @pl.when(goal == z - 1)
        def _():
            last_copy(slot, block).start()

    def depth(goal):
        last = n_tensor - 1
        return jnp.where(
            goal > z, z, jnp.where(goal < z, last - z, jnp.maximum(z, last - z))
        )

    steps = n_context * PIECES

    @pl.loop(0, steps + LAG * (n_tensor - 1))
    def _(step):
        @pl.when(step < steps)
        def _():
            owner, piece = arrival(step)
            slot, goal, block = place(owner, piece)

            @pl.when(owner > 0)
            def _():
                send_held(slot, slot, core_send.at[0], to_core).wait_recv()

            @pl.when(jnp.logical_and(owner > 0, owner % 2 == 0))
            def _():
                send_held(slot, slot + PIECES, core_send.at[owner // 2 * PIECES + piece], to_core).start()

            @pl.when(jnp.logical_and(owner == 2, piece < 2))
            def _():
                send_held(slot, 6 * PIECES + piece, y_send.at[PIECES + piece], to_y).start()

            @pl.when(jnp.logical_and(owner == 4, piece >= 2))
            def _():
                send_held(slot, 6 * PIECES + piece, x_send.at[PIECES + piece - 2], to_x).start()

            @pl.when(jnp.logical_and(owner == 2, piece == 1))
            def _():
                for late in (0, 1):
                    send_held(late, 4 * PIECES + late, y_send.at[late], to_y).start()

            @pl.when(jnp.logical_and(owner == 4, piece == 3))
            def _():
                for late in (2, 3):
                    send_held(late, 2 * PIECES + late, x_send.at[late], to_x).start()

            stage[slot] = jnp.dot(
                gated[...], held[slot], preferred_element_type=jnp.float32
            ).astype(jnp.bfloat16)

            @pl.when(depth(goal) == 0)
            def _():
                pass_on(slot, goal, block)

        for hop in range(1, n_tensor):
            event = step - hop * LAG
            owner, piece = arrival(event)
            slot, goal, block = place(owner, piece)
            due = jnp.logical_and(
                jnp.logical_and(event >= 0, event < steps), depth(goal) == hop
            )

            @pl.when(jnp.logical_and(due, goal != z))
            def _():
                up_copy(slot).wait_recv()
                stage[slot] = (
                    stage[slot].astype(jnp.float32) + main[slot].astype(jnp.float32)
                ).astype(jnp.bfloat16)
                pass_on(slot, goal, block)

            @pl.when(jnp.logical_and(due, goal == z))
            def _():
                spot = pl.ds(pl.multiple_of(block * cols, cols), cols)

                @pl.when(z == 0)
                def _():
                    last_copy(slot, block).wait_recv()
                    mixed[:, spot] = (
                        stage[slot].astype(jnp.float32) + extra[block].astype(jnp.float32)
                    ).astype(jnp.bfloat16)

                @pl.when(z == n_tensor - 1)
                def _():
                    up_copy(slot).wait_recv()
                    mixed[:, spot] = (
                        stage[slot].astype(jnp.float32) + main[slot].astype(jnp.float32)
                    ).astype(jnp.bfloat16)

                @pl.when(jnp.logical_and(z > 0, z < n_tensor - 1))
                def _():
                    up_copy(slot).wait_recv()
                    last_copy(slot, block).wait_recv()
                    mixed[:, spot] = (
                        stage[slot].astype(jnp.float32)
                        + main[slot].astype(jnp.float32)
                        + extra[block].astype(jnp.float32)
                    ).astype(jnp.bfloat16)

    local = sites[...] - c * rows
    one_hot = (
        lax.broadcasted_iota(jnp.int32, (local.shape[0], rows), 1) == local
    ).astype(jnp.float32).astype(jnp.bfloat16)
    for part in range(width // 256):
        spot = pl.ds(part * 256, 256)
        outbox[:, spot] = jnp.dot(
            one_hot, mixed[:, spot], preferred_element_type=jnp.float32
        ).astype(jnp.bfloat16)

    def pick_copy(step, target):
        return pltpu.make_async_remote_copy(
            src_ref=outbox.at[pl.ds(pl.multiple_of(target * SLOTS, SLOTS), SLOTS), :],
            dst_ref=inbox.at[step - 1],
            send_sem=pick_send.at[step - 1], recv_sem=pick_recv.at[step - 1],
            device_id={"context": target}, device_id_type=MESH,
        )

    picks = [pick_copy(step, lax.rem(c + step, n_context)) for step in range(1, n_context)]
    for copy in picks:
        copy.start()
    total = outbox[pl.ds(pl.multiple_of(c * SLOTS, SLOTS), SLOTS), :].astype(jnp.float32)
    for step, copy in enumerate(picks):
        copy.wait_recv()
        total = total + inbox[step].astype(jnp.float32)
    picked[...] = total.astype(jnp.bfloat16)

    for copy in picks:
        copy.wait_send()

    @pl.when(c < n_context - 1)
    def _():
        for copy in halo_copies(c + 1):
            copy.wait_send()

    for index in range(6):
        send_held(0, 0, x_send.at[index], to_x).wait_send()
        send_held(0, 0, y_send.at[index], to_y).wait_send()

    @pl.loop(0, 4 * PIECES)
    def _(index):
        send_held(0, 0, core_send.at[index], to_core).wait_send()

    @pl.loop(0, steps)
    def _(step):
        slot, goal, block = place(step // PIECES, step % PIECES)

        @pl.when(goal != z)
        def _():
            up_copy(slot).wait_send()


def fused_on_device(projected, taps, filters, skip, out_weight, positions):
    _, rows, width = projected.shape
    depth, mine = out_weight.shape
    cols = mine // PIECES
    n_context = lax.axis_size("context")
    sites = positions.shape[0] // n_context
    groups = filters.shape[0]
    bands = jnp.concatenate(
        [
            jnp.zeros((groups, 1), filters.dtype),
            jnp.flip(filters, axis=1),
            jnp.zeros((groups, FLT - 1), filters.dtype),
        ],
        axis=1,
    ).astype(jnp.float32)
    padded = jnp.pad(
        positions.reshape(n_context, sites), ((0, 0), (0, SLOTS - sites)), constant_values=-1
    ).reshape(n_context * SLOTS, 1)
    padded = jnp.where(padded < 0, -rows * n_context, padded)
    chunks = n_context * PIECES
    bf = jnp.bfloat16
    vmem = pl.BlockSpec(memory_space=pltpu.VMEM)
    hbm = pl.BlockSpec(memory_space=pl.ANY)
    dma = pltpu.SemaphoreType.DMA
    mixed, picked = pl.pallas_call(
        fused,
        out_shape=(
            jax.ShapeDtypeStruct((rows, 2 * mine), bf),
            jax.ShapeDtypeStruct((SLOTS, 2 * mine), bf),
        ),
        in_specs=[hbm, vmem, vmem, vmem, hbm, vmem],
        out_specs=(vmem, vmem),
        scratch_shapes=[
            pltpu.VMEM((3, HALO + rows, width), bf),
            pltpu.VMEM((chunks, depth, cols), bf),
            pltpu.VMEM((rows, width), bf),
            pltpu.VMEM((chunks, rows, cols), bf),
            pltpu.VMEM((chunks, rows, cols), bf),
            pltpu.VMEM((2 * PIECES, rows, cols), bf),
            pltpu.VMEM((n_context * SLOTS, 2 * mine), bf),
            pltpu.VMEM((n_context - 1, SLOTS, 2 * mine), bf),
            dma((PIECES + 1,)),
            dma((2,)),
            dma((2,)),
            dma((6,)),
            dma((6,)),
            dma((4 * PIECES,)),
            dma((chunks,)),
            dma((chunks,)),
            dma((chunks,)),
            dma((2 * PIECES,)),
            dma((n_context - 1,)),
            dma((n_context - 1,)),
        ],
        compiler_params=pltpu.CompilerParams(
            collective_id=0, has_side_effects=True, vmem_limit_bytes=62 * 1024 * 1024
        ),
        cost_estimate=pl.CostEstimate(
            flops=2 * rows * width * mine * n_context, bytes_accessed=2**24, transcendentals=0
        ),
    )(projected, taps, bands, skip.reshape(1, width), out_weight, padded)
    return mixed, picked[:sites]


def fits(mesh):
    return mesh.shape["context"] == 8 and mesh.shape["tensor"] == 4


def solution(mesh):
    return jax.shard_map(
        fused_on_device if fits(mesh) else on_device,
        mesh=mesh,
        in_specs=(
            P(None, "context", "tensor"),
            P(None, None, "tensor"),
            P("tensor", None),
            P("tensor"),
            P("tensor", "context"),
            P(),
        ),
        out_specs=(P("context", "tensor"), P("context", "tensor")),
        check_vma=False,
    )
```

```python
import jax
import jax.numpy as jnp
from jax import lax
from jax.experimental import pallas as pl
from jax.experimental.pallas import tpu as pltpu
from jax.sharding import PartitionSpec as P

FLT = 128
GROUP = 16
SHORT = 3


def shifted(array, axis, by):
    size = lax.axis_size(axis)
    pairs = [(i, i + by) for i in range(size) if 0 <= i + by < size]
    return lax.ppermute(array, axis, pairs)


def short_filter(extended, weights, count):
    lags = SHORT - 1
    total = jnp.zeros((extended.shape[0], count, extended.shape[2]), jnp.float32)
    for lag in range(SHORT):
        total = total + weights[:, lag, None, :] * extended[
            :, lags - lag : lags - lag + count, :
        ].astype(jnp.float32)
    return total


def banded_filters(filters, rows):
    local_groups = filters.shape[0]
    span = FLT - 1 + rows
    reversed_taps = jnp.flip(filters, axis=1)
    padded_taps = jnp.concatenate(
        [reversed_taps, jnp.zeros((local_groups, rows), filters.dtype)], axis=1
    )
    tiled = jnp.tile(padded_taps, (1, rows))
    return tiled[:, : rows * span].reshape(local_groups, rows, span)


def on_device(projected, taps, filters, skip, out_weight, positions):
    rows = projected.shape[1]
    width = projected.shape[2]
    lags = SHORT - 1
    reach = FLT - 1
    rim = shifted(projected[:, rows - lags :, :], "context", 1)
    feat = short_filter(jnp.concatenate([rim, projected], axis=1), taps, rows)
    query = feat[0]
    product = (feat[1] * feat[2]).astype(jnp.bfloat16)
    prior = shifted(product[rows - reach :], "context", 1)
    extended = jnp.concatenate([prior, product], axis=0)
    span = reach + rows
    toeplitz = banded_filters(filters, rows)
    local_groups = filters.shape[0]
    conv = jnp.einsum(
        "gim,mgc->igc",
        toeplitz,
        extended.reshape(span, local_groups, GROUP),
        preferred_element_type=jnp.float32,
    ).reshape(rows, width)
    conv = conv + skip[None, :] * product.astype(jnp.float32)
    gated = (query * conv).astype(jnp.bfloat16)
    terms = jnp.dot(
        gated,
        lax.all_gather(out_weight, "context", axis=1, tiled=True),
        preferred_element_type=jnp.float32,
    )
    mixed = lax.psum_scatter(terms.astype(jnp.bfloat16), "tensor", scatter_dimension=1, tiled=True)
    offset = lax.axis_index("context") * rows
    local_sites = positions - offset
    one_hot = (local_sites[:, None] == jnp.arange(rows, dtype=jnp.int32)[None, :]).astype(
        jnp.bfloat16
    )
    picked_terms = jnp.dot(one_hot, mixed, preferred_element_type=jnp.float32)
    variant_states = lax.psum_scatter(
        picked_terms.astype(jnp.bfloat16), "context", scatter_dimension=0, tiled=True
    )
    return (mixed, variant_states)


LANES = 128
PIECES = 2
LAG = 2
HALO = 144
RIM = 16
SLOTS = 16
MESH = pl.DeviceIdType.MESH


def flip(index, bit):
    return index + bit - 2 * bit * ((index // bit) % 2)


def arrival(step):
    early = step - 4
    round_one = step - 14
    round_two = step - 24
    first = step < 4
    swapped = step < 12
    relayed = step < 14
    ahead = step < 22
    tail = step < 24
    mixed_one = 2 * (round_one % 4) + round_one // 4
    mixed_two = 2 * (round_two % 4) + round_two // 4
    owner = jnp.where(
        first, step // 2,
        jnp.where(
            swapped, 2 + 2 * (early % 2) + early % 4 // 2,
            jnp.where(
                relayed, step - 6,
                jnp.where(ahead, mixed_one, jnp.where(tail, step - 16, mixed_two)),
            ),
        ),
    )
    piece = jnp.where(
        first, step % 2, jnp.where(swapped, early // 4, jnp.where(ahead, 0, 1))
    )
    late = jnp.where(relayed, 0, jnp.where(ahead, 1, jnp.where(tail, 0, 1)))
    return owner, piece, late


def fused(
    proj, taps, bands, skip, weight, sites, mixed, picked,
    ext, held, away, gated, stage, main, extra, outbox, inbox,
    local_sem, halo_send, halo_recv, x_send, y_send, core_send, held_recv,
    z_send, main_recv, extra_recv, pick_send, pick_recv,
    rows_send, rows_recv, out_send, out_recv,
):
    _, rows, width = gated.shape
    cols = held.shape[2]
    c = lax.axis_index("context")
    z = lax.axis_index("tensor")
    n_context = lax.axis_size("context")
    n_tensor = lax.axis_size("tensor")
    to_x, to_y, to_core = flip(c, 2), flip(c, 4), flip(c, 1)
    half = c // 2 % 2

    barrier = pltpu.get_barrier_semaphore()
    for step in range(1, n_context):
        pl.semaphore_signal(
            barrier, inc=1, device_id={"context": lax.rem(c + step, n_context)}, device_id_type=MESH
        )

    @pl.when(z > 0)
    def _():
        pl.semaphore_signal(barrier, inc=1, device_id={"tensor": z - 1}, device_id_type=MESH)

    @pl.when(z < n_tensor - 1)
    def _():
        pl.semaphore_signal(barrier, inc=1, device_id={"tensor": z + 1}, device_id_type=MESH)

    def weight_piece(side, piece):
        return weight.at[
            :, pl.ds(pl.multiple_of((side * PIECES + piece) * cols, cols), cols)
        ]

    away_copies = [
        pltpu.make_async_copy(
            weight_piece(1 - half, piece), away.at[piece], local_sem.at[piece]
        )
        for piece in range(PIECES)
    ]
    own_copies = [
        pltpu.make_async_copy(
            weight_piece(half, piece), held.at[piece], local_sem.at[PIECES + piece]
        )
        for piece in range(PIECES)
    ]
    for copy in away_copies + own_copies:
        copy.start()
    load = pltpu.make_async_copy(proj, ext.at[:, pl.ds(HALO, rows), :], local_sem.at[2 * PIECES])
    load.start()

    inner = jnp.logical_and(z > 0, z < n_tensor - 1)
    pl.semaphore_wait(barrier, n_context + jnp.where(inner, 1, 0))

    def halo_copies(target):
        return (
            pltpu.make_async_remote_copy(
                src_ref=proj.at[pl.ds(1, 2), pl.ds(rows - HALO, HALO), :],
                dst_ref=ext.at[pl.ds(1, 2), pl.ds(0, HALO), :],
                send_sem=halo_send.at[0], recv_sem=halo_recv.at[0],
                device_id={"context": target}, device_id_type=MESH,
            ),
            pltpu.make_async_remote_copy(
                src_ref=proj.at[0, pl.ds(rows - RIM, RIM), :],
                dst_ref=ext.at[0, pl.ds(HALO - RIM, RIM), :],
                send_sem=halo_send.at[1], recv_sem=halo_recv.at[1],
                device_id={"context": target}, device_id_type=MESH,
            ),
        )

    @pl.when(c < n_context - 1)
    def _():
        for copy in halo_copies(c + 1):
            copy.start()

    def send_held(source, landing, send_sem, target):
        return pltpu.make_async_remote_copy(
            src_ref=held.at[source], dst_ref=held.at[landing],
            send_sem=send_sem, recv_sem=held_recv.at[landing],
            device_id={"context": target}, device_id_type=MESH,
        )

    def send_away(piece):
        return pltpu.make_async_remote_copy(
            src_ref=away.at[piece], dst_ref=held.at[2 * PIECES + piece],
            send_sem=x_send.at[piece], recv_sem=held_recv.at[2 * PIECES + piece],
            device_id={"context": to_x}, device_id_type=MESH,
        )

    for piece in range(PIECES):
        away_copies[piece].wait()
        send_away(piece).start()
        own_copies[piece].wait()
        send_held(piece, 4 * PIECES + piece, y_send.at[piece], to_y).start()
    for piece in range(PIECES):
        send_held(piece, PIECES + piece, core_send.at[piece], to_core).start()

    load.wait()

    @pl.when(c == 0)
    def _():
        ext[:, pl.ds(0, HALO), :] = jnp.zeros((3, HALO, width), ext.dtype)

    @pl.when(c > 0)
    def _():
        for copy in halo_copies(c):
            copy.wait_recv()

    blocks = rows // FLT
    per_tile = LANES // GROUP

    @pl.loop(0, width // LANES)
    def _(tile):
        lanes = pl.ds(pl.multiple_of(tile * LANES, LANES), LANES)

        def feature(which, start):
            values = ext[which, pl.ds(start - RIM, HALO + rows - start + RIM), lanes].astype(jnp.float32)
            count = values.shape[0] - RIM
            weights = taps[which, :, lanes]
            total = weights[0:1] * values[RIM:]
            for lag in range(1, SHORT):
                total = total + weights[lag : lag + 1] * values[RIM - lag : RIM - lag + count]
            return total

        query = feature(0, HALO)
        product = (feature(1, RIM) * feature(2, RIM)).astype(jnp.bfloat16)
        wide = jnp.concatenate(
            [product[b * FLT : (b + 2) * FLT] for b in range(blocks)], axis=1
        )
        group_of = lax.broadcasted_iota(jnp.int32, (FLT, blocks * LANES), 1) % LANES // GROUP
        total = jnp.zeros((FLT, blocks * LANES), jnp.float32)
        for g in range(per_tile):
            row = bands[pl.ds(tile * per_tile + g, 1), :]
            band = pltpu.roll(
                jnp.broadcast_to(row, (FLT, 2 * FLT)), 0, 1, stride=1, stride_axis=0
            ).astype(jnp.bfloat16)
            term = jnp.dot(band, wide, preferred_element_type=jnp.float32)
            total = jnp.where(group_of == g, term, total)
        direct = skip[:, lanes]
        for b in range(blocks):
            here = product[(b + 1) * FLT : (b + 2) * FLT].astype(jnp.float32)
            conv = total[:, b * LANES : (b + 1) * LANES] + direct * here
            gated[0, pl.ds(b * FLT, FLT), lanes] = (
                query[b * FLT : (b + 1) * FLT] * conv
            ).astype(jnp.bfloat16)

    rows_copy = pltpu.make_async_remote_copy(
        src_ref=gated.at[0], dst_ref=gated.at[1],
        send_sem=rows_send.at[0], recv_sem=rows_recv.at[0],
        device_id={"context": to_x}, device_id_type=MESH,
    )
    rows_copy.start()

    def place(owner, piece, late):
        up_y = (c // 4 + owner // 4) % 2
        up_x = (c // 2 + owner // 2) % 2
        up_core = (c + owner) % 2
        slot = (late * n_context + owner) * PIECES + piece
        block = (late * 2 + up_core) * PIECES + piece
        return slot, 2 * up_y + up_x, block

    def spot_of(block, side):
        core = block // PIECES % 2
        index = (core * 2 + side) * PIECES + block % PIECES
        return pl.ds(pl.multiple_of(index * cols, cols), cols)

    def out_copy(slot, block):
        spot = spot_of(block, half)
        lane = block % (2 * PIECES)
        return pltpu.make_async_remote_copy(
            src_ref=stage.at[slot], dst_ref=mixed.at[:, spot],
            send_sem=out_send.at[lane], recv_sem=out_recv.at[lane],
            device_id={"context": to_x}, device_id_type=MESH,
        )

    def up_copy(slot):
        return pltpu.make_async_remote_copy(
            src_ref=stage.at[slot], dst_ref=main.at[slot],
            send_sem=z_send.at[slot], recv_sem=main_recv.at[slot],
            device_id={"tensor": z + 1}, device_id_type=MESH,
        )

    def down_copy(slot):
        return pltpu.make_async_remote_copy(
            src_ref=stage.at[slot], dst_ref=main.at[slot],
            send_sem=z_send.at[slot], recv_sem=main_recv.at[slot],
            device_id={"tensor": z - 1}, device_id_type=MESH,
        )

    def last_copy(slot, block):
        return pltpu.make_async_remote_copy(
            src_ref=stage.at[slot], dst_ref=extra.at[block],
            send_sem=z_send.at[slot], recv_sem=extra_recv.at[block],
            device_id={"tensor": z - 1}, device_id_type=MESH,
        )

    def pass_on(slot, goal, block):
        @pl.when(goal > z)
        def _():
            up_copy(slot).start()

        @pl.when(goal < z - 1)
        def _():
            down_copy(slot).start()

        @pl.when(goal == z - 1)
        def _():
            last_copy(slot, block).start()

    def depth(goal):
        last = n_tensor - 1
        return jnp.where(
            goal > z, z, jnp.where(goal < z, last - z, jnp.maximum(z, last - z))
        )

    steps = 2 * n_context * PIECES

    @pl.loop(0, steps + LAG * (n_tensor - 1))
    def _(step):
        @pl.when(step < steps)
        def _():
            owner, piece, late = arrival(step)
            slot, goal, block = place(owner, piece, late)
            chunk = owner * PIECES + piece

            @pl.when(jnp.logical_and(late == 0, owner > 0))
            def _():
                send_held(chunk, chunk, core_send.at[0], to_core).wait_recv()

            @pl.when(jnp.logical_and(late == 0, jnp.logical_and(owner > 0, owner % 2 == 0)))
            def _():
                send_held(
                    chunk, chunk + PIECES, core_send.at[owner // 2 * PIECES + piece], to_core
                ).start()

            @pl.when(jnp.logical_and(late == 0, owner == 2))
            def _():
                send_held(chunk, 6 * PIECES + piece, y_send.at[PIECES + piece], to_y).start()

            @pl.when(step == 14)
            def _():
                rows_copy.wait_recv()

            stage[slot] = jnp.dot(
                gated[late], held[chunk], preferred_element_type=jnp.float32
            ).astype(jnp.bfloat16)

            @pl.when(depth(goal) == 0)
            def _():
                pass_on(slot, goal, block)

        for hop in range(1, n_tensor):
            event = step - hop * LAG
            owner, piece, late = arrival(event)
            slot, goal, block = place(owner, piece, late)
            due = jnp.logical_and(
                jnp.logical_and(event >= 0, event < steps), depth(goal) == hop
            )

            @pl.when(jnp.logical_and(due, goal != z))
            def _():
                up_copy(slot).wait_recv()
                stage[slot] = (
                    stage[slot].astype(jnp.float32) + main[slot].astype(jnp.float32)
                ).astype(jnp.bfloat16)
                pass_on(slot, goal, block)

            @pl.when(jnp.logical_and(due, goal == z))
            def _():
                @pl.when(z < n_tensor - 1)
                def _():
                    last_copy(slot, block).wait_recv()

                @pl.when(z > 0)
                def _():
                    up_copy(slot).wait_recv()

                def finish(result):
                    @pl.when(late == 0)
                    def _():
                        mixed[:, spot_of(block, half)] = result

                    @pl.when(late == 1)
                    def _():
                        stage[slot] = result
                        out_copy(slot, block).start()

                @pl.when(z == 0)
                def _():
                    finish((
                        stage[slot].astype(jnp.float32) + extra[block].astype(jnp.float32)
                    ).astype(jnp.bfloat16))

                @pl.when(z == n_tensor - 1)
                def _():
                    finish((
                        stage[slot].astype(jnp.float32) + main[slot].astype(jnp.float32)
                    ).astype(jnp.bfloat16))

                @pl.when(jnp.logical_and(z > 0, z < n_tensor - 1))
                def _():
                    finish((
                        stage[slot].astype(jnp.float32)
                        + main[slot].astype(jnp.float32)
                        + extra[block].astype(jnp.float32)
                    ).astype(jnp.bfloat16))

    for lane in range(2 * PIECES):
        pltpu.make_async_remote_copy(
            src_ref=stage.at[0], dst_ref=mixed.at[:, spot_of(lane, 1 - half)],
            send_sem=out_send.at[lane], recv_sem=out_recv.at[lane],
            device_id={"context": to_x}, device_id_type=MESH,
        ).wait_recv()

    local = sites[...] - c * rows
    one_hot = (
        lax.broadcasted_iota(jnp.int32, (local.shape[0], rows), 1) == local
    ).astype(jnp.float32).astype(jnp.bfloat16)
    for part in range(width // 256):
        spot = pl.ds(part * 256, 256)
        outbox[:, spot] = jnp.dot(
            one_hot, mixed[:, spot], preferred_element_type=jnp.float32
        ).astype(jnp.bfloat16)

    def pick_copy(step, target):
        return pltpu.make_async_remote_copy(
            src_ref=outbox.at[pl.ds(pl.multiple_of(target * SLOTS, SLOTS), SLOTS), :],
            dst_ref=inbox.at[step - 1],
            send_sem=pick_send.at[step - 1], recv_sem=pick_recv.at[step - 1],
            device_id={"context": target}, device_id_type=MESH,
        )

    picks = [pick_copy(step, lax.rem(c + step, n_context)) for step in range(1, n_context)]
    for copy in picks:
        copy.start()
    total = outbox[pl.ds(pl.multiple_of(c * SLOTS, SLOTS), SLOTS), :].astype(jnp.float32)
    for step, copy in enumerate(picks):
        copy.wait_recv()
        total = total + inbox[step].astype(jnp.float32)
    picked[...] = total.astype(jnp.bfloat16)

    for copy in picks:
        copy.wait_send()

    @pl.when(c < n_context - 1)
    def _():
        for copy in halo_copies(c + 1):
            copy.wait_send()

    rows_copy.wait_send()
    for piece in range(PIECES):
        send_away(piece).wait_send()
    for index in range(2 * PIECES):
        send_held(0, 0, y_send.at[index], to_y).wait_send()
        out_copy(0, index).wait_send()

    @pl.loop(0, 4 * PIECES)
    def _(index):
        send_held(0, 0, core_send.at[index], to_core).wait_send()

    @pl.loop(0, steps)
    def _(step):
        owner, piece, late = arrival(step)
        slot, goal, block = place(owner, piece, late)

        @pl.when(goal != z)
        def _():
            up_copy(slot).wait_send()


def fused_on_device(projected, taps, filters, skip, out_weight, positions):
    _, rows, width = projected.shape
    depth, mine = out_weight.shape
    cols = mine // (2 * PIECES)
    n_context = lax.axis_size("context")
    sites = positions.shape[0] // n_context
    groups = filters.shape[0]
    bands = jnp.concatenate(
        [
            jnp.zeros((groups, 1), filters.dtype),
            jnp.flip(filters, axis=1),
            jnp.zeros((groups, FLT - 1), filters.dtype),
        ],
        axis=1,
    ).astype(jnp.float32)
    padded = jnp.pad(
        positions.reshape(n_context, sites), ((0, 0), (0, SLOTS - sites)), constant_values=-1
    ).reshape(n_context * SLOTS, 1)
    padded = jnp.where(padded < 0, -rows * n_context, padded)
    chunks = n_context * PIECES
    bf = jnp.bfloat16
    vmem = pl.BlockSpec(memory_space=pltpu.VMEM)
    hbm = pl.BlockSpec(memory_space=pl.ANY)
    dma = pltpu.SemaphoreType.DMA
    mixed, picked = pl.pallas_call(
        fused,
        out_shape=(
            jax.ShapeDtypeStruct((rows, 2 * mine), bf),
            jax.ShapeDtypeStruct((SLOTS, 2 * mine), bf),
        ),
        in_specs=[hbm, vmem, vmem, vmem, hbm, vmem],
        out_specs=(vmem, vmem),
        scratch_shapes=[
            pltpu.VMEM((3, HALO + rows, width), bf),
            pltpu.VMEM((chunks, depth, cols), bf),
            pltpu.VMEM((PIECES, depth, cols), bf),
            pltpu.VMEM((2, rows, width), bf),
            pltpu.VMEM((2 * chunks, rows, cols), bf),
            pltpu.VMEM((2 * chunks, rows, cols), bf),
            pltpu.VMEM((4 * PIECES, rows, cols), bf),
            pltpu.VMEM((n_context * SLOTS, 2 * mine), bf),
            pltpu.VMEM((n_context - 1, SLOTS, 2 * mine), bf),
            dma((2 * PIECES + 1,)),
            dma((2,)),
            dma((2,)),
            dma((PIECES,)),
            dma((2 * PIECES,)),
            dma((4 * PIECES,)),
            dma((chunks,)),
            dma((2 * chunks,)),
            dma((2 * chunks,)),
            dma((4 * PIECES,)),
            dma((n_context - 1,)),
            dma((n_context - 1,)),
            dma((1,)),
            dma((1,)),
            dma((2 * PIECES,)),
            dma((2 * PIECES,)),
        ],
        compiler_params=pltpu.CompilerParams(
            collective_id=0, has_side_effects=True, vmem_limit_bytes=62 * 1024 * 1024
        ),
        cost_estimate=pl.CostEstimate(
            flops=2 * rows * width * mine * n_context, bytes_accessed=2**24, transcendentals=0
        ),
    )(projected, taps, bands, skip.reshape(1, width), out_weight, padded)
    return mixed, picked[:sites]


def fits(mesh):
    return mesh.shape["context"] == 8 and mesh.shape["tensor"] == 4


def solution(mesh):
    return jax.shard_map(
        fused_on_device if fits(mesh) else on_device,
        mesh=mesh,
        in_specs=(
            P(None, "context", "tensor"),
            P(None, None, "tensor"),
            P("tensor", None),
            P("tensor"),
            P("tensor", "context"),
            P(),
        ),
        out_specs=(P("context", "tensor"), P("context", "tensor")),
        check_vma=False,
    )
```

```python
import jax
import jax.numpy as jnp
from jax import lax
from jax.experimental import pallas as pl
from jax.experimental.pallas import tpu as pltpu
from jax.sharding import PartitionSpec as P

FLT = 128
GROUP = 16
SHORT = 3


def shifted(array, axis, by):
    size = lax.axis_size(axis)
    pairs = [(i, i + by) for i in range(size) if 0 <= i + by < size]
    return lax.ppermute(array, axis, pairs)


def short_filter(extended, weights, count):
    lags = SHORT - 1
    total = jnp.zeros((extended.shape[0], count, extended.shape[2]), jnp.float32)
    for lag in range(SHORT):
        total = total + weights[:, lag, None, :] * extended[
            :, lags - lag : lags - lag + count, :
        ].astype(jnp.float32)
    return total


def banded_filters(filters, rows):
    local_groups = filters.shape[0]
    span = FLT - 1 + rows
    reversed_taps = jnp.flip(filters, axis=1)
    padded_taps = jnp.concatenate(
        [reversed_taps, jnp.zeros((local_groups, rows), filters.dtype)], axis=1
    )
    tiled = jnp.tile(padded_taps, (1, rows))
    return tiled[:, : rows * span].reshape(local_groups, rows, span)


def on_device(projected, taps, filters, skip, out_weight, positions):
    rows = projected.shape[1]
    width = projected.shape[2]
    lags = SHORT - 1
    reach = FLT - 1
    rim = shifted(projected[:, rows - lags :, :], "context", 1)
    feat = short_filter(jnp.concatenate([rim, projected], axis=1), taps, rows)
    query = feat[0]
    product = (feat[1] * feat[2]).astype(jnp.bfloat16)
    prior = shifted(product[rows - reach :], "context", 1)
    extended = jnp.concatenate([prior, product], axis=0)
    span = reach + rows
    toeplitz = banded_filters(filters, rows)
    local_groups = filters.shape[0]
    conv = jnp.einsum(
        "gim,mgc->igc",
        toeplitz,
        extended.reshape(span, local_groups, GROUP),
        preferred_element_type=jnp.float32,
    ).reshape(rows, width)
    conv = conv + skip[None, :] * product.astype(jnp.float32)
    gated = (query * conv).astype(jnp.bfloat16)
    terms = jnp.dot(
        gated,
        lax.all_gather(out_weight, "context", axis=1, tiled=True),
        preferred_element_type=jnp.float32,
    )
    mixed = lax.psum_scatter(terms.astype(jnp.bfloat16), "tensor", scatter_dimension=1, tiled=True)
    offset = lax.axis_index("context") * rows
    local_sites = positions - offset
    one_hot = (local_sites[:, None] == jnp.arange(rows, dtype=jnp.int32)[None, :]).astype(
        jnp.bfloat16
    )
    picked_terms = jnp.dot(one_hot, mixed, preferred_element_type=jnp.float32)
    variant_states = lax.psum_scatter(
        picked_terms.astype(jnp.bfloat16), "context", scatter_dimension=0, tiled=True
    )
    return (mixed, variant_states)


LANES = 128
PIECES = 2
LAG = 3
HALO = 144
RIM = 16
SLOTS = 16
MESH = pl.DeviceIdType.MESH


def flip(index, bit):
    return index + bit - 2 * bit * ((index // bit) % 2)


def arrival(step):
    early = step - 4
    round_one = step - 14
    round_two = step - 24
    first = step < 4
    swapped = step < 12
    relayed = step < 14
    ahead = step < 22
    tail = step < 24
    mixed_one = 2 * (round_one % 4) + round_one // 4
    mixed_two = 2 * (round_two % 4) + round_two // 4
    owner = jnp.where(
        first, step // 2,
        jnp.where(
            swapped, 2 + 2 * (early % 2) + early % 4 // 2,
            jnp.where(
                relayed, step - 6,
                jnp.where(ahead, mixed_one, jnp.where(tail, step - 16, mixed_two)),
            ),
        ),
    )
    piece = jnp.where(
        first, step % 2, jnp.where(swapped, early // 4, jnp.where(ahead, 0, 1))
    )
    late = jnp.where(relayed, 0, jnp.where(ahead, 1, jnp.where(tail, 0, 1)))
    return owner, piece, late


def fused(
    proj, taps, filters, skip, weight, sites, mixed, picked,
    ext, base, bands, held, away, gated, stage, main, extra, outbox, inbox,
    local_sem, halo_send, halo_recv, x_send, y_send, core_send, held_recv,
    z_send, main_recv, extra_recv, pick_send, pick_recv,
    rows_send, rows_recv, out_send, out_recv,
):
    _, rows, width = gated.shape
    cols = held.shape[2]
    c = lax.axis_index("context")
    z = lax.axis_index("tensor")
    n_context = lax.axis_size("context")
    n_tensor = lax.axis_size("tensor")
    to_x, to_y, to_core = flip(c, 2), flip(c, 4), flip(c, 1)
    half = c // 2 % 2

    barrier = pltpu.get_barrier_semaphore()
    for step in range(1, n_context):
        pl.semaphore_signal(
            barrier, inc=1, device_id={"context": lax.rem(c + step, n_context)}, device_id_type=MESH
        )

    @pl.when(z > 0)
    def _():
        pl.semaphore_signal(barrier, inc=1, device_id={"tensor": z - 1}, device_id_type=MESH)

    @pl.when(z < n_tensor - 1)
    def _():
        pl.semaphore_signal(barrier, inc=1, device_id={"tensor": z + 1}, device_id_type=MESH)

    def weight_piece(side, piece):
        return weight.at[
            :, pl.ds(pl.multiple_of((side * PIECES + piece) * cols, cols), cols)
        ]

    away_copies = [
        pltpu.make_async_copy(
            weight_piece(1 - half, piece), away.at[piece], local_sem.at[piece]
        )
        for piece in range(PIECES)
    ]
    own_copies = [
        pltpu.make_async_copy(
            weight_piece(half, piece), held.at[piece], local_sem.at[PIECES + piece]
        )
        for piece in range(PIECES)
    ]
    for copy in away_copies + own_copies:
        copy.start()
    load = pltpu.make_async_copy(proj, ext.at[:, pl.ds(HALO, rows), :], local_sem.at[2 * PIECES])
    load.start()

    inner = jnp.logical_and(z > 0, z < n_tensor - 1)
    pl.semaphore_wait(barrier, n_context + jnp.where(inner, 1, 0))

    def halo_copies(target):
        return (
            pltpu.make_async_remote_copy(
                src_ref=proj.at[pl.ds(1, 2), pl.ds(rows - HALO, HALO), :],
                dst_ref=ext.at[pl.ds(1, 2), pl.ds(0, HALO), :],
                send_sem=halo_send.at[0], recv_sem=halo_recv.at[0],
                device_id={"context": target}, device_id_type=MESH,
            ),
            pltpu.make_async_remote_copy(
                src_ref=proj.at[0, pl.ds(rows - RIM, RIM), :],
                dst_ref=ext.at[0, pl.ds(HALO - RIM, RIM), :],
                send_sem=halo_send.at[1], recv_sem=halo_recv.at[1],
                device_id={"context": target}, device_id_type=MESH,
            ),
        )

    @pl.when(c < n_context - 1)
    def _():
        for copy in halo_copies(c + 1):
            copy.start()

    shape = (FLT, 2 * FLT)
    mirror = (
        lax.broadcasted_iota(jnp.int32, shape, 0) + lax.broadcasted_iota(jnp.int32, shape, 1) == FLT
    ).astype(jnp.float32).astype(jnp.bfloat16)
    base[...] = jnp.dot(filters[...], mirror, preferred_element_type=jnp.float32)

    @pl.loop(0, filters.shape[0] // 8)
    def _(octet):
        taken = base[pl.ds(pl.multiple_of(octet * 8, 8), 8), :]
        for g in range(8):
            row = jnp.broadcast_to(taken[g : g + 1], shape)
            bands[octet * 8 + g] = pltpu.roll(row, 0, 1, stride=1, stride_axis=0).astype(
                jnp.bfloat16
            )

    def send_held(source, landing, send_sem, target):
        return pltpu.make_async_remote_copy(
            src_ref=held.at[source], dst_ref=held.at[landing],
            send_sem=send_sem, recv_sem=held_recv.at[landing],
            device_id={"context": target}, device_id_type=MESH,
        )

    def send_away(piece):
        return pltpu.make_async_remote_copy(
            src_ref=away.at[piece], dst_ref=held.at[2 * PIECES + piece],
            send_sem=x_send.at[piece], recv_sem=held_recv.at[2 * PIECES + piece],
            device_id={"context": to_x}, device_id_type=MESH,
        )

    for piece in range(PIECES):
        away_copies[piece].wait()
        send_away(piece).start()
        own_copies[piece].wait()
        send_held(piece, 4 * PIECES + piece, y_send.at[piece], to_y).start()
    for piece in range(PIECES):
        send_held(piece, PIECES + piece, core_send.at[piece], to_core).start()

    load.wait()

    @pl.when(c == 0)
    def _():
        ext[:, pl.ds(0, HALO), :] = jnp.zeros((3, HALO, width), ext.dtype)

    @pl.when(c > 0)
    def _():
        for copy in halo_copies(c):
            copy.wait_recv()

    blocks = rows // FLT
    per_tile = LANES // GROUP

    @pl.loop(0, width // LANES)
    def _(tile):
        lanes = pl.ds(pl.multiple_of(tile * LANES, LANES), LANES)

        def feature(which, start):
            values = ext[which, pl.ds(start - RIM, HALO + rows - start + RIM), lanes].astype(jnp.float32)
            count = values.shape[0] - RIM
            weights = taps[which, :, lanes]
            total = weights[0:1] * values[RIM:]
            for lag in range(1, SHORT):
                total = total + weights[lag : lag + 1] * values[RIM - lag : RIM - lag + count]
            return total

        query = feature(0, HALO)
        product = (feature(1, RIM) * feature(2, RIM)).astype(jnp.bfloat16)
        wide = jnp.concatenate(
            [product[b * FLT : (b + 2) * FLT] for b in range(blocks)], axis=1
        )
        group_of = lax.broadcasted_iota(jnp.int32, (FLT, blocks * LANES), 1) % LANES // GROUP
        total = jnp.zeros((FLT, blocks * LANES), jnp.float32)
        for g in range(per_tile):
            band = bands[tile * per_tile + g]
            term = jnp.dot(band, wide, preferred_element_type=jnp.float32)
            total = jnp.where(group_of == g, term, total)
        direct = skip[:, lanes]
        for b in range(blocks):
            here = product[(b + 1) * FLT : (b + 2) * FLT].astype(jnp.float32)
            conv = total[:, b * LANES : (b + 1) * LANES] + direct * here
            gated[0, pl.ds(b * FLT, FLT), lanes] = (
                query[b * FLT : (b + 1) * FLT] * conv
            ).astype(jnp.bfloat16)

    rows_copy = pltpu.make_async_remote_copy(
        src_ref=gated.at[0], dst_ref=gated.at[1],
        send_sem=rows_send.at[0], recv_sem=rows_recv.at[0],
        device_id={"context": to_x}, device_id_type=MESH,
    )
    rows_copy.start()

    def place(owner, piece, late):
        up_y = (c // 4 + owner // 4) % 2
        up_x = (c // 2 + owner // 2) % 2
        up_core = (c + owner) % 2
        slot = (late * n_context + owner) * PIECES + piece
        block = (late * 2 + up_core) * PIECES + piece
        return slot, 2 * up_y + up_x, block

    def spot_of(block, side):
        core = block // PIECES % 2
        index = (core * 2 + side) * PIECES + block % PIECES
        return pl.ds(pl.multiple_of(index * cols, cols), cols)

    def out_copy(slot, block):
        spot = spot_of(block, half)
        lane = block % (2 * PIECES)
        return pltpu.make_async_remote_copy(
            src_ref=stage.at[slot], dst_ref=mixed.at[:, spot],
            send_sem=out_send.at[lane], recv_sem=out_recv.at[lane],
            device_id={"context": to_x}, device_id_type=MESH,
        )

    def up_copy(slot):
        return pltpu.make_async_remote_copy(
            src_ref=stage.at[slot], dst_ref=main.at[slot],
            send_sem=z_send.at[slot], recv_sem=main_recv.at[slot],
            device_id={"tensor": z + 1}, device_id_type=MESH,
        )

    def down_copy(slot):
        return pltpu.make_async_remote_copy(
            src_ref=stage.at[slot], dst_ref=main.at[slot],
            send_sem=z_send.at[slot], recv_sem=main_recv.at[slot],
            device_id={"tensor": z - 1}, device_id_type=MESH,
        )

    def last_copy(slot, block):
        return pltpu.make_async_remote_copy(
            src_ref=stage.at[slot], dst_ref=extra.at[block],
            send_sem=z_send.at[slot], recv_sem=extra_recv.at[block],
            device_id={"tensor": z - 1}, device_id_type=MESH,
        )

    def pass_on(slot, goal, block):
        @pl.when(goal > z)
        def _():
            up_copy(slot).start()

        @pl.when(goal < z - 1)
        def _():
            down_copy(slot).start()

        @pl.when(goal == z - 1)
        def _():
            last_copy(slot, block).start()

    def depth(goal):
        last = n_tensor - 1
        return jnp.where(
            goal > z, z, jnp.where(goal < z, last - z, jnp.maximum(z, last - z))
        )

    steps = 2 * n_context * PIECES

    @pl.loop(0, steps + LAG * (n_tensor - 1))
    def _(step):
        @pl.when(step < steps)
        def _():
            owner, piece, late = arrival(step)
            slot, goal, block = place(owner, piece, late)
            chunk = owner * PIECES + piece

            @pl.when(jnp.logical_and(late == 0, owner > 0))
            def _():
                send_held(chunk, chunk, core_send.at[0], to_core).wait_recv()

            @pl.when(jnp.logical_and(late == 0, jnp.logical_and(owner > 0, owner % 2 == 0)))
            def _():
                send_held(
                    chunk, chunk + PIECES, core_send.at[owner // 2 * PIECES + piece], to_core
                ).start()

            @pl.when(jnp.logical_and(late == 0, owner == 2))
            def _():
                send_held(chunk, 6 * PIECES + piece, y_send.at[PIECES + piece], to_y).start()

            @pl.when(step == 14)
            def _():
                rows_copy.wait_recv()

            stage[slot] = jnp.dot(
                gated[late], held[chunk], preferred_element_type=jnp.float32
            ).astype(jnp.bfloat16)

            @pl.when(depth(goal) == 0)
            def _():
                pass_on(slot, goal, block)

        for hop in range(1, n_tensor):
            event = step - hop * LAG
            owner, piece, late = arrival(event)
            slot, goal, block = place(owner, piece, late)
            due = jnp.logical_and(
                jnp.logical_and(event >= 0, event < steps), depth(goal) == hop
            )

            @pl.when(jnp.logical_and(due, goal != z))
            def _():
                up_copy(slot).wait_recv()
                stage[slot] = (
                    stage[slot].astype(jnp.float32) + main[slot].astype(jnp.float32)
                ).astype(jnp.bfloat16)
                pass_on(slot, goal, block)

            @pl.when(jnp.logical_and(due, goal == z))
            def _():
                @pl.when(z < n_tensor - 1)
                def _():
                    last_copy(slot, block).wait_recv()

                @pl.when(z > 0)
                def _():
                    up_copy(slot).wait_recv()

                def finish(result):
                    @pl.when(late == 0)
                    def _():
                        mixed[:, spot_of(block, half)] = result

                    @pl.when(late == 1)
                    def _():
                        stage[slot] = result
                        out_copy(slot, block).start()

                @pl.when(z == 0)
                def _():
                    finish((
                        stage[slot].astype(jnp.float32) + extra[block].astype(jnp.float32)
                    ).astype(jnp.bfloat16))

                @pl.when(z == n_tensor - 1)
                def _():
                    finish((
                        stage[slot].astype(jnp.float32) + main[slot].astype(jnp.float32)
                    ).astype(jnp.bfloat16))

                @pl.when(jnp.logical_and(z > 0, z < n_tensor - 1))
                def _():
                    finish((
                        stage[slot].astype(jnp.float32)
                        + main[slot].astype(jnp.float32)
                        + extra[block].astype(jnp.float32)
                    ).astype(jnp.bfloat16))

    for lane in range(2 * PIECES):
        pltpu.make_async_remote_copy(
            src_ref=stage.at[0], dst_ref=mixed.at[:, spot_of(lane, 1 - half)],
            send_sem=out_send.at[lane], recv_sem=out_recv.at[lane],
            device_id={"context": to_x}, device_id_type=MESH,
        ).wait_recv()

    count = sites.shape[0]
    each = count // n_context
    row_at = lax.broadcasted_iota(jnp.int32, (n_context * SLOTS, 1), 0)
    local = jnp.full((n_context * SLOTS, 1), -1, jnp.int32)
    for v in range(count):
        local = jnp.where(
            row_at == v // each * SLOTS + v % each, sites[v] - c * rows, local
        )
    one_hot = (
        lax.broadcasted_iota(jnp.int32, (n_context * SLOTS, rows), 1) == local
    ).astype(jnp.float32).astype(jnp.bfloat16)
    for part in range(width // 256):
        spot = pl.ds(part * 256, 256)
        outbox[:, spot] = jnp.dot(
            one_hot, mixed[:, spot], preferred_element_type=jnp.float32
        ).astype(jnp.bfloat16)

    def pick_copy(step, target):
        return pltpu.make_async_remote_copy(
            src_ref=outbox.at[pl.ds(pl.multiple_of(target * SLOTS, SLOTS), SLOTS), :],
            dst_ref=inbox.at[step - 1],
            send_sem=pick_send.at[step - 1], recv_sem=pick_recv.at[step - 1],
            device_id={"context": target}, device_id_type=MESH,
        )

    picks = [pick_copy(step, lax.rem(c + step, n_context)) for step in range(1, n_context)]
    for copy in picks:
        copy.start()
    total = outbox[pl.ds(pl.multiple_of(c * SLOTS, SLOTS), SLOTS), :].astype(jnp.float32)
    for step, copy in enumerate(picks):
        copy.wait_recv()
        total = total + inbox[step].astype(jnp.float32)
    picked[...] = total[:each].astype(jnp.bfloat16)

    for copy in picks:
        copy.wait_send()

    @pl.when(c < n_context - 1)
    def _():
        for copy in halo_copies(c + 1):
            copy.wait_send()

    rows_copy.wait_send()
    for piece in range(PIECES):
        send_away(piece).wait_send()
    for index in range(2 * PIECES):
        send_held(0, 0, y_send.at[index], to_y).wait_send()
        out_copy(0, index).wait_send()

    @pl.loop(0, 4 * PIECES)
    def _(index):
        send_held(0, 0, core_send.at[index], to_core).wait_send()

    @pl.loop(0, steps)
    def _(step):
        owner, piece, late = arrival(step)
        slot, goal, block = place(owner, piece, late)

        @pl.when(goal != z)
        def _():
            up_copy(slot).wait_send()


def fused_on_device(projected, taps, filters, skip, out_weight, positions):
    _, rows, width = projected.shape
    depth, mine = out_weight.shape
    cols = mine // (2 * PIECES)
    n_context = lax.axis_size("context")
    sites = positions.shape[0] // n_context
    groups = filters.shape[0]
    chunks = n_context * PIECES
    bf = jnp.bfloat16
    vmem = pl.BlockSpec(memory_space=pltpu.VMEM)
    hbm = pl.BlockSpec(memory_space=pl.ANY)
    dma = pltpu.SemaphoreType.DMA
    mixed, picked = pl.pallas_call(
        fused,
        out_shape=(
            jax.ShapeDtypeStruct((rows, 2 * mine), bf),
            jax.ShapeDtypeStruct((sites, 2 * mine), bf),
        ),
        in_specs=[
            hbm, vmem, vmem, vmem, hbm, pl.BlockSpec(memory_space=pltpu.SMEM)
        ],
        out_specs=(vmem, vmem),
        scratch_shapes=[
            pltpu.VMEM((3, HALO + rows, width), bf),
            pltpu.VMEM((groups, 2 * FLT), jnp.float32),
            pltpu.VMEM((groups, FLT, 2 * FLT), bf),
            pltpu.VMEM((chunks, depth, cols), bf),
            pltpu.VMEM((PIECES, depth, cols), bf),
            pltpu.VMEM((2, rows, width), bf),
            pltpu.VMEM((2 * chunks, rows, cols), bf),
            pltpu.VMEM((2 * chunks, rows, cols), bf),
            pltpu.VMEM((4 * PIECES, rows, cols), bf),
            pltpu.VMEM((n_context * SLOTS, 2 * mine), bf),
            pltpu.VMEM((n_context - 1, SLOTS, 2 * mine), bf),
            dma((2 * PIECES + 1,)),
            dma((2,)),
            dma((2,)),
            dma((PIECES,)),
            dma((2 * PIECES,)),
            dma((4 * PIECES,)),
            dma((chunks,)),
            dma((2 * chunks,)),
            dma((2 * chunks,)),
            dma((4 * PIECES,)),
            dma((n_context - 1,)),
            dma((n_context - 1,)),
            dma((1,)),
            dma((1,)),
            dma((2 * PIECES,)),
            dma((2 * PIECES,)),
        ],
        compiler_params=pltpu.CompilerParams(
            collective_id=0, has_side_effects=True, vmem_limit_bytes=62 * 1024 * 1024
        ),
        cost_estimate=pl.CostEstimate(
            flops=2 * rows * width * mine * n_context, bytes_accessed=2**24, transcendentals=0
        ),
    )(projected, taps, filters, skip.reshape(1, width), out_weight, positions)
    return mixed, picked


def fits(mesh):
    return mesh.shape["context"] == 8 and mesh.shape["tensor"] == 4


def solution(mesh):
    return jax.shard_map(
        fused_on_device if fits(mesh) else on_device,
        mesh=mesh,
        in_specs=(
            P(None, "context", "tensor"),
            P(None, None, "tensor"),
            P("tensor", None),
            P("tensor"),
            P("tensor", "context"),
            P(),
        ),
        out_specs=(P("context", "tensor"), P("context", "tensor")),
        check_vma=False,
    )
```

```python
import jax
import jax.numpy as jnp
from jax import lax
from jax.experimental import pallas as pl
from jax.experimental.pallas import tpu as pltpu
from jax.sharding import PartitionSpec as P

FLT = 128
GROUP = 16
SHORT = 3


def shifted(array, axis, by):
    size = lax.axis_size(axis)
    pairs = [(i, i + by) for i in range(size) if 0 <= i + by < size]
    return lax.ppermute(array, axis, pairs)


def short_filter(extended, weights, count):
    lags = SHORT - 1
    total = jnp.zeros((extended.shape[0], count, extended.shape[2]), jnp.float32)
    for lag in range(SHORT):
        total = total + weights[:, lag, None, :] * extended[
            :, lags - lag : lags - lag + count, :
        ].astype(jnp.float32)
    return total


def banded_filters(filters, rows):
    local_groups = filters.shape[0]
    span = FLT - 1 + rows
    reversed_taps = jnp.flip(filters, axis=1)
    padded_taps = jnp.concatenate(
        [reversed_taps, jnp.zeros((local_groups, rows), filters.dtype)], axis=1
    )
    tiled = jnp.tile(padded_taps, (1, rows))
    return tiled[:, : rows * span].reshape(local_groups, rows, span)


def on_device(projected, taps, filters, skip, out_weight, positions):
    rows = projected.shape[1]
    width = projected.shape[2]
    lags = SHORT - 1
    reach = FLT - 1
    rim = shifted(projected[:, rows - lags :, :], "context", 1)
    feat = short_filter(jnp.concatenate([rim, projected], axis=1), taps, rows)
    query = feat[0]
    product = (feat[1] * feat[2]).astype(jnp.bfloat16)
    prior = shifted(product[rows - reach :], "context", 1)
    extended = jnp.concatenate([prior, product], axis=0)
    span = reach + rows
    toeplitz = banded_filters(filters, rows)
    local_groups = filters.shape[0]
    conv = jnp.einsum(
        "gim,mgc->igc",
        toeplitz,
        extended.reshape(span, local_groups, GROUP),
        preferred_element_type=jnp.float32,
    ).reshape(rows, width)
    conv = conv + skip[None, :] * product.astype(jnp.float32)
    gated = (query * conv).astype(jnp.bfloat16)
    terms = jnp.dot(
        gated,
        lax.all_gather(out_weight, "context", axis=1, tiled=True),
        preferred_element_type=jnp.float32,
    )
    mixed = lax.psum_scatter(terms.astype(jnp.bfloat16), "tensor", scatter_dimension=1, tiled=True)
    offset = lax.axis_index("context") * rows
    local_sites = positions - offset
    one_hot = (local_sites[:, None] == jnp.arange(rows, dtype=jnp.int32)[None, :]).astype(
        jnp.bfloat16
    )
    picked_terms = jnp.dot(one_hot, mixed, preferred_element_type=jnp.float32)
    variant_states = lax.psum_scatter(
        picked_terms.astype(jnp.bfloat16), "context", scatter_dimension=0, tiled=True
    )
    return (mixed, variant_states)


LANES = 128
PIECES = 2
LAG = 3
HALO = 144
RIM = 16
SLOTS = 16
MESH = pl.DeviceIdType.MESH


def flip(index, bit):
    return index + bit - 2 * bit * ((index // bit) % 2)


ORDER = (
    (0, 0, 0), (0, 1, 0), (1, 0, 0), (1, 1, 0), (2, 0, 0), (4, 0, 0), (3, 0, 0), (5, 0, 0),
    (4, 1, 0), (5, 1, 0), (0, 0, 1), (0, 1, 1), (1, 0, 1), (1, 1, 1), (2, 0, 1), (4, 0, 1),
    (3, 0, 1), (5, 0, 1), (4, 1, 1), (5, 1, 1), (6, 0, 1), (7, 0, 1), (6, 0, 0), (7, 0, 0),
    (2, 1, 1), (3, 1, 1), (2, 1, 0), (3, 1, 0), (6, 1, 1), (7, 1, 1), (6, 1, 0), (7, 1, 0),
)
ROWS_STEP = 10
RELAY_STEP = 18


def coded():
    seen = {(0, 0), (0, 1), (2, 1)}
    codes = []
    for owner, piece, late in ORDER:
        fresh = (owner, piece) not in seen
        seen.add((owner, piece))
        codes.append(owner * 8 + piece * 4 + late * 2 + int(fresh))
    return codes


def arrival(step):
    values = coded()
    rest = jnp.maximum(step, 0)
    while len(values) > 1:
        odd = rest % 2 == 1
        values = [jnp.where(odd, b, a) for a, b in zip(values[::2], values[1::2])]
        rest = rest // 2
    code = values[0]
    return code // 8, code // 4 % 2, code // 2 % 2, code % 2


def fused(
    proj, taps, filters, skip, weight, sites, mixed, picked,
    ext, base, bands, held, away, gated, stage, main, extra, outbox, inbox,
    local_sem, halo_send, halo_recv, x_send, y_send, core_send, held_recv,
    z_send, main_recv, extra_recv, pick_send, pick_recv,
    rows_send, rows_recv, out_send, out_recv,
):
    _, rows, width = gated.shape
    cols = held.shape[2]
    c = lax.axis_index("context")
    z = lax.axis_index("tensor")
    n_context = lax.axis_size("context")
    n_tensor = lax.axis_size("tensor")
    to_x, to_y, to_core = flip(c, 2), flip(c, 4), flip(c, 1)
    half = c // 2 % 2

    barrier = pltpu.get_barrier_semaphore()
    for step in range(1, n_context):
        pl.semaphore_signal(
            barrier, inc=1, device_id={"context": lax.rem(c + step, n_context)}, device_id_type=MESH
        )

    @pl.when(z > 0)
    def _():
        pl.semaphore_signal(barrier, inc=1, device_id={"tensor": z - 1}, device_id_type=MESH)

    @pl.when(z < n_tensor - 1)
    def _():
        pl.semaphore_signal(barrier, inc=1, device_id={"tensor": z + 1}, device_id_type=MESH)

    def weight_piece(side, piece):
        return weight.at[
            :, pl.ds(pl.multiple_of((side * PIECES + piece) * cols, cols), cols)
        ]

    away_copies = [
        pltpu.make_async_copy(
            weight_piece(1 - half, piece), away.at[piece], local_sem.at[piece]
        )
        for piece in range(PIECES)
    ]
    own_copies = [
        pltpu.make_async_copy(
            weight_piece(half, piece), held.at[piece], local_sem.at[PIECES + piece]
        )
        for piece in range(PIECES)
    ]
    for copy in away_copies + own_copies:
        copy.start()
    load = pltpu.make_async_copy(proj, ext.at[:, pl.ds(HALO, rows), :], local_sem.at[2 * PIECES])
    load.start()

    inner = jnp.logical_and(z > 0, z < n_tensor - 1)
    pl.semaphore_wait(barrier, n_context + jnp.where(inner, 1, 0))

    def halo_copies(target):
        return (
            pltpu.make_async_remote_copy(
                src_ref=proj.at[pl.ds(1, 2), pl.ds(rows - HALO, HALO), :],
                dst_ref=ext.at[pl.ds(1, 2), pl.ds(0, HALO), :],
                send_sem=halo_send.at[0], recv_sem=halo_recv.at[0],
                device_id={"context": target}, device_id_type=MESH,
            ),
            pltpu.make_async_remote_copy(
                src_ref=proj.at[0, pl.ds(rows - RIM, RIM), :],
                dst_ref=ext.at[0, pl.ds(HALO - RIM, RIM), :],
                send_sem=halo_send.at[1], recv_sem=halo_recv.at[1],
                device_id={"context": target}, device_id_type=MESH,
            ),
        )

    @pl.when(c < n_context - 1)
    def _():
        for copy in halo_copies(c + 1):
            copy.start()

    shape = (FLT, 2 * FLT)
    mirror = (
        lax.broadcasted_iota(jnp.int32, shape, 0) + lax.broadcasted_iota(jnp.int32, shape, 1) == FLT
    ).astype(jnp.float32).astype(jnp.bfloat16)
    base[...] = jnp.dot(filters[...], mirror, preferred_element_type=jnp.float32)

    @pl.loop(0, filters.shape[0] // 8)
    def _(octet):
        taken = base[pl.ds(pl.multiple_of(octet * 8, 8), 8), :]
        for g in range(8):
            row = jnp.broadcast_to(taken[g : g + 1], shape)
            start = pl.multiple_of((octet * 8 + g) * FLT, FLT)
            bands[pl.ds(start, FLT), :] = pltpu.roll(
                row, 0, 1, stride=1, stride_axis=0
            ).astype(jnp.bfloat16)

    def send_held(source, landing, send_sem, target):
        return pltpu.make_async_remote_copy(
            src_ref=held.at[source], dst_ref=held.at[landing],
            send_sem=send_sem, recv_sem=held_recv.at[landing],
            device_id={"context": target}, device_id_type=MESH,
        )

    def send_away(piece):
        return pltpu.make_async_remote_copy(
            src_ref=away.at[piece], dst_ref=held.at[2 * PIECES + piece],
            send_sem=x_send.at[piece], recv_sem=held_recv.at[2 * PIECES + piece],
            device_id={"context": to_x}, device_id_type=MESH,
        )

    for piece in range(PIECES):
        away_copies[piece].wait()
        if piece == 0:
            send_away(piece).start()
        own_copies[piece].wait()
        send_held(piece, 4 * PIECES + piece, y_send.at[piece], to_y).start()
    for piece in range(PIECES):
        send_held(piece, PIECES + piece, core_send.at[piece], to_core).start()

    load.wait()

    @pl.when(c == 0)
    def _():
        ext[:, pl.ds(0, HALO), :] = jnp.zeros((3, HALO, width), ext.dtype)

    @pl.when(c > 0)
    def _():
        for copy in halo_copies(c):
            copy.wait_recv()

    blocks = rows // FLT
    per_tile = LANES // GROUP

    @pl.loop(0, width // LANES)
    def _(tile):
        lanes = pl.ds(pl.multiple_of(tile * LANES, LANES), LANES)

        def feature(which, start):
            values = ext[which, pl.ds(start - RIM, HALO + rows - start + RIM), lanes].astype(jnp.float32)
            count = values.shape[0] - RIM
            weights = taps[which, :, lanes]
            total = weights[0:1] * values[RIM:]
            for lag in range(1, SHORT):
                total = total + weights[lag : lag + 1] * values[RIM - lag : RIM - lag + count]
            return total

        query = feature(0, HALO)
        product = (feature(1, RIM) * feature(2, RIM)).astype(jnp.bfloat16)
        wide = jnp.concatenate(
            [product[b * FLT : (b + 2) * FLT] for b in range(blocks)], axis=1
        )
        group_of = lax.broadcasted_iota(jnp.int32, (FLT, blocks * LANES), 1) % LANES // GROUP
        start = pl.multiple_of(tile * (per_tile * FLT), per_tile * FLT)
        terms = jnp.dot(
            bands[pl.ds(start, per_tile * FLT), :], wide, preferred_element_type=jnp.float32
        )
        total = terms[:FLT]
        for g in range(1, per_tile):
            total = jnp.where(group_of == g, terms[g * FLT : (g + 1) * FLT], total)
        direct = skip[:, lanes]
        for b in range(blocks):
            here = product[(b + 1) * FLT : (b + 2) * FLT].astype(jnp.float32)
            conv = total[:, b * LANES : (b + 1) * LANES] + direct * here
            gated[0, pl.ds(b * FLT, FLT), lanes] = (
                query[b * FLT : (b + 1) * FLT] * conv
            ).astype(jnp.bfloat16)

    rows_copy = pltpu.make_async_remote_copy(
        src_ref=gated.at[0], dst_ref=gated.at[1],
        send_sem=rows_send.at[0], recv_sem=rows_recv.at[0],
        device_id={"context": to_x}, device_id_type=MESH,
    )
    rows_copy.start()

    def place(owner, piece, late):
        up_y = (c // 4 + owner // 4) % 2
        up_x = (c // 2 + owner // 2) % 2
        up_core = (c + owner) % 2
        slot = (late * n_context + owner) * PIECES + piece
        block = (late * 2 + up_core) * PIECES + piece
        return slot, 2 * up_y + up_x, block

    def spot_of(block, side):
        core = block // PIECES % 2
        index = (core * 2 + side) * PIECES + block % PIECES
        return pl.ds(pl.multiple_of(index * cols, cols), cols)

    def out_copy(slot, block):
        spot = spot_of(block, half)
        lane = block % (2 * PIECES)
        return pltpu.make_async_remote_copy(
            src_ref=stage.at[slot], dst_ref=mixed.at[:, spot],
            send_sem=out_send.at[lane], recv_sem=out_recv.at[lane],
            device_id={"context": to_x}, device_id_type=MESH,
        )

    def up_copy(slot):
        return pltpu.make_async_remote_copy(
            src_ref=stage.at[slot], dst_ref=main.at[slot],
            send_sem=z_send.at[slot], recv_sem=main_recv.at[slot],
            device_id={"tensor": z + 1}, device_id_type=MESH,
        )

    def down_copy(slot):
        return pltpu.make_async_remote_copy(
            src_ref=stage.at[slot], dst_ref=main.at[slot],
            send_sem=z_send.at[slot], recv_sem=main_recv.at[slot],
            device_id={"tensor": z - 1}, device_id_type=MESH,
        )

    def last_copy(slot, block):
        return pltpu.make_async_remote_copy(
            src_ref=stage.at[slot], dst_ref=extra.at[block],
            send_sem=z_send.at[slot], recv_sem=extra_recv.at[block],
            device_id={"tensor": z - 1}, device_id_type=MESH,
        )

    def pass_on(slot, goal, block):
        @pl.when(goal > z)
        def _():
            up_copy(slot).start()

        @pl.when(goal < z - 1)
        def _():
            down_copy(slot).start()

        @pl.when(goal == z - 1)
        def _():
            last_copy(slot, block).start()

    def depth(goal):
        last = n_tensor - 1
        return jnp.where(
            goal > z, z, jnp.where(goal < z, last - z, jnp.maximum(z, last - z))
        )

    steps = 2 * n_context * PIECES

    @pl.loop(0, steps + LAG * (n_tensor - 1))
    def _(step):
        @pl.when(step < steps)
        def _():
            owner, piece, late, fresh = arrival(step)
            slot, goal, block = place(owner, piece, late)
            chunk = owner * PIECES + piece

            @pl.when(fresh == 1)
            def _():
                send_held(chunk, chunk, core_send.at[0], to_core).wait_recv()

            @pl.when(jnp.logical_and(fresh == 1, owner % 2 == 0))
            def _():
                send_held(
                    chunk, chunk + PIECES, core_send.at[owner // 2 * PIECES + piece], to_core
                ).start()

            @pl.when(jnp.logical_and(fresh == 1, owner == 2))
            def _():
                send_held(chunk, 6 * PIECES + piece, y_send.at[PIECES + piece], to_y).start()

            @pl.when(step == RELAY_STEP)
            def _():
                swapped = 2 * PIECES + 1
                send_away(1).wait_recv()
                send_held(swapped, 6 * PIECES + 1, y_send.at[PIECES + 1], to_y).start()
                send_held(swapped, 3 * PIECES + 1, core_send.at[PIECES + 1], to_core).start()

            @pl.when(step == ROWS_STEP)
            def _():
                rows_copy.wait_recv()
                send_away(1).start()

            stage[slot] = jnp.dot(
                gated[late], held[chunk], preferred_element_type=jnp.float32
            ).astype(jnp.bfloat16)

            @pl.when(depth(goal) == 0)
            def _():
                pass_on(slot, goal, block)

        for hop in range(1, n_tensor):
            event = step - hop * LAG
            owner, piece, late, _ = arrival(event)
            slot, goal, block = place(owner, piece, late)
            due = jnp.logical_and(
                jnp.logical_and(event >= 0, event < steps), depth(goal) == hop
            )

            @pl.when(jnp.logical_and(due, goal != z))
            def _():
                up_copy(slot).wait_recv()
                stage[slot] = (
                    stage[slot].astype(jnp.float32) + main[slot].astype(jnp.float32)
                ).astype(jnp.bfloat16)
                pass_on(slot, goal, block)

            @pl.when(jnp.logical_and(due, goal == z))
            def _():
                @pl.when(z < n_tensor - 1)
                def _():
                    last_copy(slot, block).wait_recv()

                @pl.when(z > 0)
                def _():
                    up_copy(slot).wait_recv()

                def finish(result):
                    @pl.when(late == 0)
                    def _():
                        mixed[:, spot_of(block, half)] = result

                    @pl.when(late == 1)
                    def _():
                        stage[slot] = result
                        out_copy(slot, block).start()

                @pl.when(z == 0)
                def _():
                    finish((
                        stage[slot].astype(jnp.float32) + extra[block].astype(jnp.float32)
                    ).astype(jnp.bfloat16))

                @pl.when(z == n_tensor - 1)
                def _():
                    finish((
                        stage[slot].astype(jnp.float32) + main[slot].astype(jnp.float32)
                    ).astype(jnp.bfloat16))

                @pl.when(jnp.logical_and(z > 0, z < n_tensor - 1))
                def _():
                    finish((
                        stage[slot].astype(jnp.float32)
                        + main[slot].astype(jnp.float32)
                        + extra[block].astype(jnp.float32)
                    ).astype(jnp.bfloat16))

    for lane in range(2 * PIECES):
        pltpu.make_async_remote_copy(
            src_ref=stage.at[0], dst_ref=mixed.at[:, spot_of(lane, 1 - half)],
            send_sem=out_send.at[lane], recv_sem=out_recv.at[lane],
            device_id={"context": to_x}, device_id_type=MESH,
        ).wait_recv()

    count = sites.shape[0]
    each = count // n_context
    row_at = lax.broadcasted_iota(jnp.int32, (n_context * SLOTS, 1), 0)
    local = jnp.full((n_context * SLOTS, 1), -1, jnp.int32)
    for v in range(count):
        local = jnp.where(
            row_at == v // each * SLOTS + v % each, sites[v] - c * rows, local
        )
    one_hot = (
        lax.broadcasted_iota(jnp.int32, (n_context * SLOTS, rows), 1) == local
    ).astype(jnp.float32).astype(jnp.bfloat16)
    for part in range(width // 256):
        spot = pl.ds(part * 256, 256)
        outbox[:, spot] = jnp.dot(
            one_hot, mixed[:, spot], preferred_element_type=jnp.float32
        ).astype(jnp.bfloat16)

    def pick_copy(step, target):
        return pltpu.make_async_remote_copy(
            src_ref=outbox.at[pl.ds(pl.multiple_of(target * SLOTS, SLOTS), SLOTS), :],
            dst_ref=inbox.at[step - 1],
            send_sem=pick_send.at[step - 1], recv_sem=pick_recv.at[step - 1],
            device_id={"context": target}, device_id_type=MESH,
        )

    picks = [pick_copy(step, lax.rem(c + step, n_context)) for step in range(1, n_context)]
    for copy in picks:
        copy.start()
    total = outbox[pl.ds(pl.multiple_of(c * SLOTS, SLOTS), SLOTS), :].astype(jnp.float32)
    for step, copy in enumerate(picks):
        copy.wait_recv()
        total = total + inbox[step].astype(jnp.float32)
    picked[...] = total[:each].astype(jnp.bfloat16)

    for copy in picks:
        copy.wait_send()

    @pl.when(c < n_context - 1)
    def _():
        for copy in halo_copies(c + 1):
            copy.wait_send()

    rows_copy.wait_send()
    for piece in range(PIECES):
        send_away(piece).wait_send()
    for index in range(2 * PIECES):
        send_held(0, 0, y_send.at[index], to_y).wait_send()
        out_copy(0, index).wait_send()

    @pl.loop(0, 4 * PIECES)
    def _(index):
        send_held(0, 0, core_send.at[index], to_core).wait_send()

    @pl.loop(0, steps)
    def _(step):
        owner, piece, late, _ = arrival(step)
        slot, goal, block = place(owner, piece, late)

        @pl.when(goal != z)
        def _():
            up_copy(slot).wait_send()


def fused_on_device(projected, taps, filters, skip, out_weight, positions):
    _, rows, width = projected.shape
    depth, mine = out_weight.shape
    cols = mine // (2 * PIECES)
    n_context = lax.axis_size("context")
    sites = positions.shape[0] // n_context
    groups = filters.shape[0]
    chunks = n_context * PIECES
    bf = jnp.bfloat16
    vmem = pl.BlockSpec(memory_space=pltpu.VMEM)
    hbm = pl.BlockSpec(memory_space=pl.ANY)
    dma = pltpu.SemaphoreType.DMA
    mixed, picked = pl.pallas_call(
        fused,
        out_shape=(
            jax.ShapeDtypeStruct((rows, 2 * mine), bf),
            jax.ShapeDtypeStruct((sites, 2 * mine), bf),
        ),
        in_specs=[
            hbm, vmem, vmem, vmem, hbm, pl.BlockSpec(memory_space=pltpu.SMEM)
        ],
        out_specs=(vmem, vmem),
        scratch_shapes=[
            pltpu.VMEM((3, HALO + rows, width), bf),
            pltpu.VMEM((groups, 2 * FLT), jnp.float32),
            pltpu.VMEM((groups * FLT, 2 * FLT), bf),
            pltpu.VMEM((chunks, depth, cols), bf),
            pltpu.VMEM((PIECES, depth, cols), bf),
            pltpu.VMEM((2, rows, width), bf),
            pltpu.VMEM((2 * chunks, rows, cols), bf),
            pltpu.VMEM((2 * chunks, rows, cols), bf),
            pltpu.VMEM((4 * PIECES, rows, cols), bf),
            pltpu.VMEM((n_context * SLOTS, 2 * mine), bf),
            pltpu.VMEM((n_context - 1, SLOTS, 2 * mine), bf),
            dma((2 * PIECES + 1,)),
            dma((2,)),
            dma((2,)),
            dma((PIECES,)),
            dma((2 * PIECES,)),
            dma((4 * PIECES,)),
            dma((chunks,)),
            dma((2 * chunks,)),
            dma((2 * chunks,)),
            dma((4 * PIECES,)),
            dma((n_context - 1,)),
            dma((n_context - 1,)),
            dma((1,)),
            dma((1,)),
            dma((2 * PIECES,)),
            dma((2 * PIECES,)),
        ],
        compiler_params=pltpu.CompilerParams(
            collective_id=0, has_side_effects=True, vmem_limit_bytes=62 * 1024 * 1024
        ),
        cost_estimate=pl.CostEstimate(
            flops=2 * rows * width * mine * n_context, bytes_accessed=2**24, transcendentals=0
        ),
    )(projected, taps, filters, skip.reshape(1, width), out_weight, positions)
    return mixed, picked


def fits(mesh):
    return mesh.shape["context"] == 8 and mesh.shape["tensor"] == 4


def solution(mesh):
    return jax.shard_map(
        fused_on_device if fits(mesh) else on_device,
        mesh=mesh,
        in_specs=(
            P(None, "context", "tensor"),
            P(None, None, "tensor"),
            P("tensor", None),
            P("tensor"),
            P("tensor", "context"),
            P(),
        ),
        out_specs=(P("context", "tensor"), P("context", "tensor")),
        check_vma=False,
    )
```

```python
import jax
import jax.numpy as jnp
from jax import lax
from jax.experimental import pallas as pl
from jax.experimental.pallas import tpu as pltpu
from jax.sharding import PartitionSpec as P

FLT = 128
GROUP = 16
SHORT = 3


def shifted(array, axis, by):
    size = lax.axis_size(axis)
    pairs = [(i, i + by) for i in range(size) if 0 <= i + by < size]
    return lax.ppermute(array, axis, pairs)


def short_filter(extended, weights, count):
    lags = SHORT - 1
    total = jnp.zeros((extended.shape[0], count, extended.shape[2]), jnp.float32)
    for lag in range(SHORT):
        total = total + weights[:, lag, None, :] * extended[
            :, lags - lag : lags - lag + count, :
        ].astype(jnp.float32)
    return total


def banded_filters(filters, rows):
    local_groups = filters.shape[0]
    span = FLT - 1 + rows
    reversed_taps = jnp.flip(filters, axis=1)
    padded_taps = jnp.concatenate(
        [reversed_taps, jnp.zeros((local_groups, rows), filters.dtype)], axis=1
    )
    tiled = jnp.tile(padded_taps, (1, rows))
    return tiled[:, : rows * span].reshape(local_groups, rows, span)


def on_device(projected, taps, filters, skip, out_weight, positions):
    rows = projected.shape[1]
    width = projected.shape[2]
    lags = SHORT - 1
    reach = FLT - 1
    rim = shifted(projected[:, rows - lags :, :], "context", 1)
    feat = short_filter(jnp.concatenate([rim, projected], axis=1), taps, rows)
    query = feat[0]
    product = (feat[1] * feat[2]).astype(jnp.bfloat16)
    prior = shifted(product[rows - reach :], "context", 1)
    extended = jnp.concatenate([prior, product], axis=0)
    span = reach + rows
    toeplitz = banded_filters(filters, rows)
    local_groups = filters.shape[0]
    conv = jnp.einsum(
        "gim,mgc->igc",
        toeplitz,
        extended.reshape(span, local_groups, GROUP),
        preferred_element_type=jnp.float32,
    ).reshape(rows, width)
    conv = conv + skip[None, :] * product.astype(jnp.float32)
    gated = (query * conv).astype(jnp.bfloat16)
    terms = jnp.dot(
        gated,
        lax.all_gather(out_weight, "context", axis=1, tiled=True),
        preferred_element_type=jnp.float32,
    )
    mixed = lax.psum_scatter(terms.astype(jnp.bfloat16), "tensor", scatter_dimension=1, tiled=True)
    offset = lax.axis_index("context") * rows
    local_sites = positions - offset
    one_hot = (local_sites[:, None] == jnp.arange(rows, dtype=jnp.int32)[None, :]).astype(
        jnp.bfloat16
    )
    picked_terms = jnp.dot(one_hot, mixed, preferred_element_type=jnp.float32)
    variant_states = lax.psum_scatter(
        picked_terms.astype(jnp.bfloat16), "context", scatter_dimension=0, tiled=True
    )
    return (mixed, variant_states)


LANES = 128
PIECES = 2
LAG = 3
HALO = 144
RIM = 16
SLOTS = 16
MESH = pl.DeviceIdType.MESH


def flip(index, bit):
    return index + bit - 2 * bit * ((index // bit) % 2)


ORDER = (
    (0, 0, 0), (0, 1, 0), (1, 0, 0), (1, 1, 0), (2, 0, 0), (4, 0, 0), (3, 0, 0), (5, 0, 0),
    (4, 1, 0), (5, 1, 0), (0, 0, 1), (0, 1, 1), (1, 0, 1), (1, 1, 1), (2, 0, 1), (4, 0, 1),
    (3, 0, 1), (5, 0, 1), (4, 1, 1), (5, 1, 1), (6, 0, 1), (7, 0, 1), (6, 0, 0), (7, 0, 0),
    (2, 1, 1), (3, 1, 1), (6, 1, 1), (2, 1, 0), (7, 1, 1), (3, 1, 0), (6, 1, 0), (7, 1, 0),
)
EARLY = 4
ROWS_STEP = 10
RELAY_STEP = 18


def coded():
    seen = {(0, 0), (0, 1), (1, 0), (1, 1), (2, 1)}
    codes = []
    for owner, piece, late in ORDER:
        fresh = (owner, piece) not in seen
        seen.add((owner, piece))
        codes.append(owner * 8 + piece * 4 + late * 2 + int(fresh))
    return codes


def arrival(step):
    values = coded()
    rest = jnp.maximum(step, 0)
    while len(values) > 1:
        odd = rest % 2 == 1
        values = [jnp.where(odd, b, a) for a, b in zip(values[::2], values[1::2])]
        rest = rest // 2
    code = values[0]
    return code // 8, code // 4 % 2, code // 2 % 2, code % 2


def fused(
    proj, taps, filters, skip, weight, sites, mixed, picked,
    ext, base, bands, held, away, gated, stage, main, extra, outbox, inbox,
    local_sem, halo_send, halo_recv, x_send, y_send, core_send, held_recv,
    z_send, main_recv, extra_recv, pick_send, pick_recv,
    rows_send, rows_recv, out_send, out_recv,
):
    _, rows, width = gated.shape
    cols = held.shape[2]
    c = lax.axis_index("context")
    z = lax.axis_index("tensor")
    n_context = lax.axis_size("context")
    n_tensor = lax.axis_size("tensor")
    to_x, to_y, to_core = flip(c, 2), flip(c, 4), flip(c, 1)
    half = c // 2 % 2

    barrier = pltpu.get_barrier_semaphore()
    for step in range(1, n_context):
        pl.semaphore_signal(
            barrier, inc=1, device_id={"context": lax.rem(c + step, n_context)}, device_id_type=MESH
        )

    @pl.when(z > 0)
    def _():
        pl.semaphore_signal(barrier, inc=1, device_id={"tensor": z - 1}, device_id_type=MESH)

    @pl.when(z < n_tensor - 1)
    def _():
        pl.semaphore_signal(barrier, inc=1, device_id={"tensor": z + 1}, device_id_type=MESH)

    def weight_piece(side, piece):
        return weight.at[
            :, pl.ds(pl.multiple_of((side * PIECES + piece) * cols, cols), cols)
        ]

    away_copies = [
        pltpu.make_async_copy(
            weight_piece(1 - half, piece), away.at[piece], local_sem.at[piece]
        )
        for piece in range(PIECES)
    ]
    own_copies = [
        pltpu.make_async_copy(
            weight_piece(half, piece), held.at[piece], local_sem.at[PIECES + piece]
        )
        for piece in range(PIECES)
    ]
    for copy in away_copies + own_copies:
        copy.start()
    load = pltpu.make_async_copy(proj, ext.at[:, pl.ds(HALO, rows), :], local_sem.at[2 * PIECES])
    load.start()

    inner = jnp.logical_and(z > 0, z < n_tensor - 1)
    pl.semaphore_wait(barrier, n_context + jnp.where(inner, 1, 0))

    def halo_copies(target):
        return (
            pltpu.make_async_remote_copy(
                src_ref=proj.at[:, pl.ds(rows - RIM, RIM), :],
                dst_ref=ext.at[:, pl.ds(HALO - RIM, RIM), :],
                send_sem=halo_send.at[1], recv_sem=halo_recv.at[1],
                device_id={"context": target}, device_id_type=MESH,
            ),
            pltpu.make_async_remote_copy(
                src_ref=proj.at[pl.ds(1, 2), pl.ds(rows - HALO, HALO - RIM), :],
                dst_ref=ext.at[pl.ds(1, 2), pl.ds(0, HALO - RIM), :],
                send_sem=halo_send.at[0], recv_sem=halo_recv.at[0],
                device_id={"context": target}, device_id_type=MESH,
            ),
        )

    @pl.when(c < n_context - 1)
    def _():
        for copy in halo_copies(c + 1):
            copy.start()

    shape = (FLT, 2 * FLT)
    mirror = (
        lax.broadcasted_iota(jnp.int32, shape, 0) + lax.broadcasted_iota(jnp.int32, shape, 1) == FLT
    ).astype(jnp.float32).astype(jnp.bfloat16)
    base[...] = jnp.dot(filters[...], mirror, preferred_element_type=jnp.float32)

    @pl.loop(0, filters.shape[0] // 8)
    def _(octet):
        taken = base[pl.ds(pl.multiple_of(octet * 8, 8), 8), :]
        for g in range(8):
            row = jnp.broadcast_to(taken[g : g + 1], shape)
            start = pl.multiple_of((octet * 8 + g) * FLT, FLT)
            bands[pl.ds(start, FLT), :] = pltpu.roll(
                row, 0, 1, stride=1, stride_axis=0
            ).astype(jnp.bfloat16)

    def send_held(source, landing, send_sem, target):
        return pltpu.make_async_remote_copy(
            src_ref=held.at[source], dst_ref=held.at[landing],
            send_sem=send_sem, recv_sem=held_recv.at[landing],
            device_id={"context": target}, device_id_type=MESH,
        )

    def send_away(piece):
        return pltpu.make_async_remote_copy(
            src_ref=away.at[piece], dst_ref=held.at[2 * PIECES + piece],
            send_sem=x_send.at[piece], recv_sem=held_recv.at[2 * PIECES + piece],
            device_id={"context": to_x}, device_id_type=MESH,
        )

    for piece in range(PIECES):
        away_copies[piece].wait()
        if piece == 0:
            send_away(piece).start()
        own_copies[piece].wait()
        send_held(piece, 4 * PIECES + piece, y_send.at[piece], to_y).start()
    for piece in range(PIECES):
        send_held(piece, PIECES + piece, core_send.at[piece], to_core).start()

    load.wait()

    @pl.when(c == 0)
    def _():
        ext[:, pl.ds(0, HALO), :] = jnp.zeros((3, HALO, width), ext.dtype)

    @pl.when(c > 0)
    def _():
        halo_copies(c)[0].wait_recv()

    blocks = rows // FLT
    per_tile = LANES // GROUP

    def convolve(tile, low, high):
        lanes = pl.ds(pl.multiple_of(tile * LANES, LANES), LANES)

        def feature(which, start):
            stop = HALO + high * FLT
            values = ext[which, pl.ds(start - RIM, stop - start + RIM), lanes].astype(jnp.float32)
            count = values.shape[0] - RIM
            weights = taps[which, :, lanes]
            total = weights[0:1] * values[RIM:]
            for lag in range(1, SHORT):
                total = total + weights[lag : lag + 1] * values[RIM - lag : RIM - lag + count]
            return total

        query = feature(0, HALO + low * FLT)
        before = RIM + low * FLT
        product = (feature(1, before) * feature(2, before)).astype(jnp.bfloat16)
        wide = jnp.concatenate(
            [product[b * FLT : (b + 2) * FLT] for b in range(high - low)], axis=1
        )
        group_of = lax.broadcasted_iota(jnp.int32, (FLT, (high - low) * LANES), 1) % LANES // GROUP
        start = pl.multiple_of(tile * (per_tile * FLT), per_tile * FLT)
        terms = jnp.dot(
            bands[pl.ds(start, per_tile * FLT), :], wide, preferred_element_type=jnp.float32
        )
        total = terms[:FLT]
        for g in range(1, per_tile):
            total = jnp.where(group_of == g, terms[g * FLT : (g + 1) * FLT], total)
        direct = skip[:, lanes]
        for b in range(high - low):
            here = product[(b + 1) * FLT : (b + 2) * FLT].astype(jnp.float32)
            conv = total[:, b * LANES : (b + 1) * LANES] + direct * here
            gated[0, pl.ds((low + b) * FLT, FLT), lanes] = (
                query[b * FLT : (b + 1) * FLT] * conv
            ).astype(jnp.bfloat16)

    @pl.loop(0, width // LANES)
    def _(tile):
        convolve(tile, 1, blocks)

    def place(owner, piece, late):
        up_y = (c // 4 + owner // 4) % 2
        up_x = (c // 2 + owner // 2) % 2
        up_core = (c + owner) % 2
        slot = (late * n_context + owner) * PIECES + piece
        block = (late * 2 + up_core) * PIECES + piece
        return slot, 2 * up_y + up_x, block

    def spot_of(block, side):
        core = block // PIECES % 2
        index = (core * 2 + side) * PIECES + block % PIECES
        return pl.ds(pl.multiple_of(index * cols, cols), cols)

    def out_copy(slot, block):
        spot = spot_of(block, half)
        lane = block % (2 * PIECES)
        return pltpu.make_async_remote_copy(
            src_ref=stage.at[slot], dst_ref=mixed.at[:, spot],
            send_sem=out_send.at[lane], recv_sem=out_recv.at[lane],
            device_id={"context": to_x}, device_id_type=MESH,
        )

    def hop_copy(slot, landing, sem, target, part):
        return pltpu.make_async_remote_copy(
            src_ref=stage.at[slot, pl.ds(*part), :], dst_ref=landing.at[pl.ds(*part), :],
            send_sem=z_send.at[slot], recv_sem=sem,
            device_id={"tensor": target}, device_id_type=MESH,
        )

    whole = (0, rows)

    def up_copy(slot, part=whole):
        return hop_copy(slot, main.at[slot], main_recv.at[slot], z + 1, part)

    def down_copy(slot, part=whole):
        return hop_copy(slot, main.at[slot], main_recv.at[slot], z - 1, part)

    def last_copy(slot, block, part=whole):
        return hop_copy(slot, extra.at[block], extra_recv.at[block], z - 1, part)

    def pass_on(slot, goal, block, part=whole):
        @pl.when(goal > z)
        def _():
            up_copy(slot, part).start()

        @pl.when(goal < z - 1)
        def _():
            down_copy(slot, part).start()

        @pl.when(goal == z - 1)
        def _():
            last_copy(slot, block, part).start()

    def depth(goal):
        last = n_tensor - 1
        return jnp.where(
            goal > z, z, jnp.where(goal < z, last - z, jnp.maximum(z, last - z))
        )

    def multiply(step, part):
        owner, piece, late, _ = arrival(step)
        slot, goal, block = place(owner, piece, late)
        stage[slot, pl.ds(*part), :] = jnp.dot(
            gated[late, pl.ds(*part), :],
            held[owner * PIECES + piece],
            preferred_element_type=jnp.float32,
        ).astype(jnp.bfloat16)

        @pl.when(depth(goal) == 0)
        def _():
            pass_on(slot, goal, block, part)

    for piece in range(PIECES):
        send_held(PIECES + piece, PIECES + piece, core_send.at[0], to_core).wait_recv()

    @pl.loop(0, EARLY)
    def _(step):
        multiply(step, (FLT, rows - FLT))

    @pl.when(c > 0)
    def _():
        halo_copies(c)[1].wait_recv()

    @pl.loop(0, width // LANES)
    def _(tile):
        convolve(tile, 0, 1)

    rows_copy = pltpu.make_async_remote_copy(
        src_ref=gated.at[0], dst_ref=gated.at[1],
        send_sem=rows_send.at[0], recv_sem=rows_recv.at[0],
        device_id={"context": to_x}, device_id_type=MESH,
    )
    rows_copy.start()

    steps = 2 * n_context * PIECES

    @pl.loop(0, steps + LAG * (n_tensor - 1))
    def _(step):
        @pl.when(step < steps)
        def _():
            owner, piece, late, fresh = arrival(step)
            slot, goal, block = place(owner, piece, late)
            chunk = owner * PIECES + piece

            @pl.when(fresh == 1)
            def _():
                send_held(chunk, chunk, core_send.at[0], to_core).wait_recv()

            @pl.when(jnp.logical_and(fresh == 1, owner % 2 == 0))
            def _():
                send_held(
                    chunk, chunk + PIECES, core_send.at[owner // 2 * PIECES + piece], to_core
                ).start()

            @pl.when(jnp.logical_and(fresh == 1, owner == 2))
            def _():
                send_held(chunk, 6 * PIECES + piece, y_send.at[PIECES + piece], to_y).start()

            @pl.when(step == RELAY_STEP)
            def _():
                swapped = 2 * PIECES + 1
                send_away(1).wait_recv()
                send_held(swapped, 6 * PIECES + 1, y_send.at[PIECES + 1], to_y).start()
                send_held(swapped, 3 * PIECES + 1, core_send.at[PIECES + 1], to_core).start()

            @pl.when(step == ROWS_STEP)
            def _():
                rows_copy.wait_recv()
                send_away(1).start()

            @pl.when(step < EARLY)
            def _():
                multiply(step, (0, FLT))

            @pl.when(step >= EARLY)
            def _():
                multiply(step, whole)

        for hop in range(1, n_tensor):
            event = step - hop * LAG
            owner, piece, late, _ = arrival(event)
            slot, goal, block = place(owner, piece, late)
            due = jnp.logical_and(
                jnp.logical_and(event >= 0, event < steps), depth(goal) == hop
            )

            @pl.when(jnp.logical_and(due, goal != z))
            def _():
                up_copy(slot).wait_recv()
                stage[slot] = (
                    stage[slot].astype(jnp.float32) + main[slot].astype(jnp.float32)
                ).astype(jnp.bfloat16)
                pass_on(slot, goal, block)

            @pl.when(jnp.logical_and(due, goal == z))
            def _():
                @pl.when(z < n_tensor - 1)
                def _():
                    last_copy(slot, block).wait_recv()

                @pl.when(z > 0)
                def _():
                    up_copy(slot).wait_recv()

                def finish(result):
                    @pl.when(late == 0)
                    def _():
                        mixed[:, spot_of(block, half)] = result

                    @pl.when(late == 1)
                    def _():
                        stage[slot] = result
                        out_copy(slot, block).start()

                @pl.when(z == 0)
                def _():
                    finish((
                        stage[slot].astype(jnp.float32) + extra[block].astype(jnp.float32)
                    ).astype(jnp.bfloat16))

                @pl.when(z == n_tensor - 1)
                def _():
                    finish((
                        stage[slot].astype(jnp.float32) + main[slot].astype(jnp.float32)
                    ).astype(jnp.bfloat16))

                @pl.when(jnp.logical_and(z > 0, z < n_tensor - 1))
                def _():
                    finish((
                        stage[slot].astype(jnp.float32)
                        + main[slot].astype(jnp.float32)
                        + extra[block].astype(jnp.float32)
                    ).astype(jnp.bfloat16))

    for lane in range(2 * PIECES):
        pltpu.make_async_remote_copy(
            src_ref=stage.at[0], dst_ref=mixed.at[:, spot_of(lane, 1 - half)],
            send_sem=out_send.at[lane], recv_sem=out_recv.at[lane],
            device_id={"context": to_x}, device_id_type=MESH,
        ).wait_recv()

    count = sites.shape[0]
    each = count // n_context
    folds = SLOTS // each
    row_at = lax.broadcasted_iota(jnp.int32, (n_context * SLOTS, 1), 0)
    local = jnp.full((n_context * SLOTS, 1), -1, jnp.int32)
    for v in range(count):
        first = v // each * SLOTS
        mine = jnp.logical_and(row_at // SLOTS * SLOTS == first, row_at % each == v % each)
        local = jnp.where(mine, sites[v] - c * rows, local)
    picks = jnp.zeros((n_context * SLOTS, outbox.shape[1]), jnp.float32)
    for fold in range(folds):
        here = jnp.where(row_at % SLOTS // each == fold, local, -1)
        one_hot = (
            lax.broadcasted_iota(jnp.int32, (n_context * SLOTS, rows), 1) == here
        ).astype(jnp.float32).astype(jnp.bfloat16)
        part = pl.ds(fold * outbox.shape[1], outbox.shape[1])
        picks = picks + jnp.dot(one_hot, mixed[:, part], preferred_element_type=jnp.float32)
    outbox[...] = picks.astype(jnp.bfloat16)

    def pick_copy(step, target):
        return pltpu.make_async_remote_copy(
            src_ref=outbox.at[pl.ds(pl.multiple_of(target * SLOTS, SLOTS), SLOTS), :],
            dst_ref=inbox.at[step - 1],
            send_sem=pick_send.at[step - 1], recv_sem=pick_recv.at[step - 1],
            device_id={"context": target}, device_id_type=MESH,
        )

    picks = [pick_copy(step, lax.rem(c + step, n_context)) for step in range(1, n_context)]
    for copy in picks:
        copy.start()
    total = outbox[pl.ds(pl.multiple_of(c * SLOTS, SLOTS), SLOTS), :].astype(jnp.float32)
    for step, copy in enumerate(picks):
        copy.wait_recv()
        total = total + inbox[step].astype(jnp.float32)
    for fold in range(folds):
        picked[:, pl.ds(fold * outbox.shape[1], outbox.shape[1])] = total[
            fold * each : (fold + 1) * each
        ].astype(jnp.bfloat16)

    for copy in picks:
        copy.wait_send()

    @pl.when(c < n_context - 1)
    def _():
        for copy in halo_copies(c + 1):
            copy.wait_send()

    rows_copy.wait_send()
    for piece in range(PIECES):
        send_away(piece).wait_send()
    for index in range(2 * PIECES):
        send_held(0, 0, y_send.at[index], to_y).wait_send()
        out_copy(0, index).wait_send()

    @pl.loop(0, 4 * PIECES)
    def _(index):
        send_held(0, 0, core_send.at[index], to_core).wait_send()

    @pl.loop(0, steps)
    def _(step):
        owner, piece, late, _ = arrival(step)
        slot, goal, block = place(owner, piece, late)

        @pl.when(goal != z)
        def _():
            up_copy(slot).wait_send()


def fused_on_device(projected, taps, filters, skip, out_weight, positions):
    _, rows, width = projected.shape
    depth, mine = out_weight.shape
    cols = mine // (2 * PIECES)
    n_context = lax.axis_size("context")
    sites = positions.shape[0] // n_context
    groups = filters.shape[0]
    chunks = n_context * PIECES
    bf = jnp.bfloat16
    vmem = pl.BlockSpec(memory_space=pltpu.VMEM)
    hbm = pl.BlockSpec(memory_space=pl.ANY)
    dma = pltpu.SemaphoreType.DMA
    mixed, picked = pl.pallas_call(
        fused,
        out_shape=(
            jax.ShapeDtypeStruct((rows, 2 * mine), bf),
            jax.ShapeDtypeStruct((sites, 2 * mine), bf),
        ),
        in_specs=[
            hbm, vmem, vmem, vmem, hbm, pl.BlockSpec(memory_space=pltpu.SMEM)
        ],
        out_specs=(vmem, vmem),
        scratch_shapes=[
            pltpu.VMEM((3, HALO + rows, width), bf),
            pltpu.VMEM((groups, 2 * FLT), jnp.float32),
            pltpu.VMEM((groups * FLT, 2 * FLT), bf),
            pltpu.VMEM((chunks, depth, cols), bf),
            pltpu.VMEM((PIECES, depth, cols), bf),
            pltpu.VMEM((2, rows, width), bf),
            pltpu.VMEM((2 * chunks, rows, cols), bf),
            pltpu.VMEM((2 * chunks, rows, cols), bf),
            pltpu.VMEM((4 * PIECES, rows, cols), bf),
            pltpu.VMEM((n_context * SLOTS, 2 * mine * sites // SLOTS), bf),
            pltpu.VMEM((n_context - 1, SLOTS, 2 * mine * sites // SLOTS), bf),
            dma((2 * PIECES + 1,)),
            dma((2,)),
            dma((2,)),
            dma((PIECES,)),
            dma((2 * PIECES,)),
            dma((4 * PIECES,)),
            dma((chunks,)),
            dma((2 * chunks,)),
            dma((2 * chunks,)),
            dma((4 * PIECES,)),
            dma((n_context - 1,)),
            dma((n_context - 1,)),
            dma((1,)),
            dma((1,)),
            dma((2 * PIECES,)),
            dma((2 * PIECES,)),
        ],
        compiler_params=pltpu.CompilerParams(
            collective_id=0, has_side_effects=True, vmem_limit_bytes=62 * 1024 * 1024
        ),
        cost_estimate=pl.CostEstimate(
            flops=2 * rows * width * mine * n_context, bytes_accessed=2**24, transcendentals=0
        ),
    )(projected, taps, filters, skip.reshape(1, width), out_weight, positions)
    return mixed, picked


def fits(mesh):
    return mesh.shape["context"] == 8 and mesh.shape["tensor"] == 4


def solution(mesh):
    return jax.shard_map(
        fused_on_device if fits(mesh) else on_device,
        mesh=mesh,
        in_specs=(
            P(None, "context", "tensor"),
            P(None, None, "tensor"),
            P("tensor", None),
            P("tensor"),
            P("tensor", "context"),
            P(),
        ),
        out_specs=(P("context", "tensor"), P("context", "tensor")),
        check_vma=False,
    )
```

```python
import jax
import jax.numpy as jnp
from jax import lax
from jax.experimental import pallas as pl
from jax.experimental.pallas import tpu as pltpu
from jax.sharding import PartitionSpec as P

FLT = 128
GROUP = 16
SHORT = 3


def shifted(array, axis, by):
    size = lax.axis_size(axis)
    pairs = [(i, i + by) for i in range(size) if 0 <= i + by < size]
    return lax.ppermute(array, axis, pairs)


def short_filter(extended, weights, count):
    lags = SHORT - 1
    total = jnp.zeros((extended.shape[0], count, extended.shape[2]), jnp.float32)
    for lag in range(SHORT):
        total = total + weights[:, lag, None, :] * extended[
            :, lags - lag : lags - lag + count, :
        ].astype(jnp.float32)
    return total


def banded_filters(filters, rows):
    local_groups = filters.shape[0]
    span = FLT - 1 + rows
    reversed_taps = jnp.flip(filters, axis=1)
    padded_taps = jnp.concatenate(
        [reversed_taps, jnp.zeros((local_groups, rows), filters.dtype)], axis=1
    )
    tiled = jnp.tile(padded_taps, (1, rows))
    return tiled[:, : rows * span].reshape(local_groups, rows, span)


def on_device(projected, taps, filters, skip, out_weight, positions):
    rows = projected.shape[1]
    width = projected.shape[2]
    lags = SHORT - 1
    reach = FLT - 1
    rim = shifted(projected[:, rows - lags :, :], "context", 1)
    feat = short_filter(jnp.concatenate([rim, projected], axis=1), taps, rows)
    query = feat[0]
    product = (feat[1] * feat[2]).astype(jnp.bfloat16)
    prior = shifted(product[rows - reach :], "context", 1)
    extended = jnp.concatenate([prior, product], axis=0)
    span = reach + rows
    toeplitz = banded_filters(filters, rows)
    local_groups = filters.shape[0]
    conv = jnp.einsum(
        "gim,mgc->igc",
        toeplitz,
        extended.reshape(span, local_groups, GROUP),
        preferred_element_type=jnp.float32,
    ).reshape(rows, width)
    conv = conv + skip[None, :] * product.astype(jnp.float32)
    gated = (query * conv).astype(jnp.bfloat16)
    terms = jnp.dot(
        gated,
        lax.all_gather(out_weight, "context", axis=1, tiled=True),
        preferred_element_type=jnp.float32,
    )
    mixed = lax.psum_scatter(terms.astype(jnp.bfloat16), "tensor", scatter_dimension=1, tiled=True)
    offset = lax.axis_index("context") * rows
    local_sites = positions - offset
    one_hot = (local_sites[:, None] == jnp.arange(rows, dtype=jnp.int32)[None, :]).astype(
        jnp.bfloat16
    )
    picked_terms = jnp.dot(one_hot, mixed, preferred_element_type=jnp.float32)
    variant_states = lax.psum_scatter(
        picked_terms.astype(jnp.bfloat16), "context", scatter_dimension=0, tiled=True
    )
    return (mixed, variant_states)


LANES = 128
PIECES = 2
LAG = 3
HALO = 144
RIM = 16
SLOTS = 16
MESH = pl.DeviceIdType.MESH


def flip(index, bit):
    return index + bit - 2 * bit * ((index // bit) % 2)


ORDER = (
    (0, 0, 0), (0, 1, 0), (1, 0, 0), (1, 1, 0), (2, 0, 0), (4, 0, 0), (3, 0, 0), (5, 0, 0),
    (4, 1, 0), (5, 1, 0), (0, 0, 1), (0, 1, 1), (1, 0, 1), (1, 1, 1), (2, 0, 1), (4, 0, 1),
    (3, 0, 1), (5, 0, 1), (4, 1, 1), (5, 1, 1), (6, 0, 1), (7, 0, 1), (6, 0, 0), (7, 0, 0),
    (2, 1, 1), (3, 1, 1), (6, 1, 1), (2, 1, 0), (7, 1, 1), (3, 1, 0), (6, 1, 0), (7, 1, 0),
)
EARLY = 4
ROWS_STEP = 10
RELAY_STEPS = (18, 21)


def coded():
    seen = {(0, 0), (0, 1), (1, 0), (1, 1), (2, 1)}
    codes = []
    for owner, piece, late in ORDER:
        fresh = (owner, piece) not in seen
        seen.add((owner, piece))
        codes.append(owner * 8 + piece * 4 + late * 2 + int(fresh))
    return codes


def arrival(step):
    values = coded()
    rest = jnp.maximum(step, 0)
    while len(values) > 1:
        odd = rest % 2 == 1
        values = [jnp.where(odd, b, a) for a, b in zip(values[::2], values[1::2])]
        rest = rest // 2
    code = values[0]
    return code // 8, code // 4 % 2, code // 2 % 2, code % 2


def fused(
    proj, taps, filters, skip, weight, sites, mixed, picked,
    ext, base, bands, held, away, gated, stage, main, extra, outbox, inbox,
    local_sem, halo_send, halo_recv, x_send, y_send, core_send, held_recv,
    z_send, main_recv, extra_recv, pick_send, pick_recv,
    rows_send, rows_recv, out_send, out_recv, half_send, half_recv, relay_send,
):
    _, rows, width = gated.shape
    cols = held.shape[2]
    c = lax.axis_index("context")
    z = lax.axis_index("tensor")
    n_context = lax.axis_size("context")
    n_tensor = lax.axis_size("tensor")
    to_x, to_y, to_core = flip(c, 2), flip(c, 4), flip(c, 1)
    half = c // 2 % 2

    barrier = pltpu.get_barrier_semaphore()
    for step in range(1, n_context):
        pl.semaphore_signal(
            barrier, inc=1, device_id={"context": lax.rem(c + step, n_context)}, device_id_type=MESH
        )

    @pl.when(z > 0)
    def _():
        pl.semaphore_signal(barrier, inc=1, device_id={"tensor": z - 1}, device_id_type=MESH)

    @pl.when(z < n_tensor - 1)
    def _():
        pl.semaphore_signal(barrier, inc=1, device_id={"tensor": z + 1}, device_id_type=MESH)

    def weight_piece(side, piece):
        return weight.at[
            :, pl.ds(pl.multiple_of((side * PIECES + piece) * cols, cols), cols)
        ]

    away_copies = [
        pltpu.make_async_copy(
            weight_piece(1 - half, piece), away.at[piece], local_sem.at[piece]
        )
        for piece in range(PIECES)
    ]
    own_copies = [
        pltpu.make_async_copy(
            weight_piece(half, piece), held.at[piece], local_sem.at[PIECES + piece]
        )
        for piece in range(PIECES)
    ]
    for copy in away_copies + own_copies:
        copy.start()
    load = pltpu.make_async_copy(proj, ext.at[:, pl.ds(HALO, rows), :], local_sem.at[2 * PIECES])
    load.start()

    inner = jnp.logical_and(z > 0, z < n_tensor - 1)
    pl.semaphore_wait(barrier, n_context + jnp.where(inner, 1, 0))

    def halo_copies(target):
        return (
            pltpu.make_async_remote_copy(
                src_ref=proj.at[:, pl.ds(rows - RIM, RIM), :],
                dst_ref=ext.at[:, pl.ds(HALO - RIM, RIM), :],
                send_sem=halo_send.at[1], recv_sem=halo_recv.at[1],
                device_id={"context": target}, device_id_type=MESH,
            ),
            pltpu.make_async_remote_copy(
                src_ref=proj.at[pl.ds(1, 2), pl.ds(rows - HALO, HALO - RIM), :],
                dst_ref=ext.at[pl.ds(1, 2), pl.ds(0, HALO - RIM), :],
                send_sem=halo_send.at[0], recv_sem=halo_recv.at[0],
                device_id={"context": target}, device_id_type=MESH,
            ),
        )

    @pl.when(c < n_context - 1)
    def _():
        for copy in halo_copies(c + 1):
            copy.start()

    shape = (FLT, 2 * FLT)
    mirror = (
        lax.broadcasted_iota(jnp.int32, shape, 0) + lax.broadcasted_iota(jnp.int32, shape, 1) == FLT
    ).astype(jnp.float32).astype(jnp.bfloat16)
    base[...] = jnp.dot(filters[...], mirror, preferred_element_type=jnp.float32)

    @pl.loop(0, filters.shape[0] // 8)
    def _(octet):
        taken = base[pl.ds(pl.multiple_of(octet * 8, 8), 8), :]
        for g in range(8):
            row = jnp.broadcast_to(taken[g : g + 1], shape)
            start = pl.multiple_of((octet * 8 + g) * FLT, FLT)
            bands[pl.ds(start, FLT), :] = pltpu.roll(
                row, 0, 1, stride=1, stride_axis=0
            ).astype(jnp.bfloat16)

    def send_held(source, landing, send_sem, target):
        return pltpu.make_async_remote_copy(
            src_ref=held.at[source], dst_ref=held.at[landing],
            send_sem=send_sem, recv_sem=held_recv.at[landing],
            device_id={"context": target}, device_id_type=MESH,
        )

    def send_away(piece):
        return pltpu.make_async_remote_copy(
            src_ref=away.at[piece], dst_ref=held.at[2 * PIECES + piece],
            send_sem=x_send.at[piece], recv_sem=held_recv.at[2 * PIECES + piece],
            device_id={"context": to_x}, device_id_type=MESH,
        )

    swapped = 2 * PIECES + 1
    deep = held.shape[1] // 2

    def send_half(part):
        span = pl.ds(part * deep, deep)
        return pltpu.make_async_remote_copy(
            src_ref=away.at[1, span, :], dst_ref=held.at[swapped, span, :],
            send_sem=half_send.at[part], recv_sem=half_recv.at[part],
            device_id={"context": to_x}, device_id_type=MESH,
        )

    def relay_half(part):
        span = pl.ds(part * deep, deep)
        return pltpu.make_async_remote_copy(
            src_ref=held.at[swapped, span, :], dst_ref=held.at[6 * PIECES + 1, span, :],
            send_sem=relay_send.at[part], recv_sem=held_recv.at[6 * PIECES + 1],
            device_id={"context": to_y}, device_id_type=MESH,
        )

    for piece in range(PIECES):
        away_copies[piece].wait()
        if piece == 0:
            send_away(piece).start()
        own_copies[piece].wait()
        send_held(piece, 4 * PIECES + piece, y_send.at[piece], to_y).start()
    for piece in range(PIECES):
        send_held(piece, PIECES + piece, core_send.at[piece], to_core).start()

    load.wait()

    @pl.when(c == 0)
    def _():
        ext[:, pl.ds(0, HALO), :] = jnp.zeros((3, HALO, width), ext.dtype)

    @pl.when(c > 0)
    def _():
        halo_copies(c)[0].wait_recv()

    blocks = rows // FLT
    per_tile = LANES // GROUP

    def convolve(tile, low, high):
        lanes = pl.ds(pl.multiple_of(tile * LANES, LANES), LANES)

        def feature(which, start):
            stop = HALO + high * FLT
            values = ext[which, pl.ds(start - RIM, stop - start + RIM), lanes].astype(jnp.float32)
            count = values.shape[0] - RIM
            weights = taps[which, :, lanes]
            total = weights[0:1] * values[RIM:]
            for lag in range(1, SHORT):
                total = total + weights[lag : lag + 1] * values[RIM - lag : RIM - lag + count]
            return total

        query = feature(0, HALO + low * FLT)
        before = RIM + low * FLT
        product = (feature(1, before) * feature(2, before)).astype(jnp.bfloat16)
        wide = jnp.concatenate(
            [product[b * FLT : (b + 2) * FLT] for b in range(high - low)], axis=1
        )
        group_of = lax.broadcasted_iota(jnp.int32, (FLT, (high - low) * LANES), 1) % LANES // GROUP
        start = pl.multiple_of(tile * (per_tile * FLT), per_tile * FLT)
        terms = jnp.dot(
            bands[pl.ds(start, per_tile * FLT), :], wide, preferred_element_type=jnp.float32
        )
        total = terms[:FLT]
        for g in range(1, per_tile):
            total = jnp.where(group_of == g, terms[g * FLT : (g + 1) * FLT], total)
        direct = skip[:, lanes]
        for b in range(high - low):
            here = product[(b + 1) * FLT : (b + 2) * FLT].astype(jnp.float32)
            conv = total[:, b * LANES : (b + 1) * LANES] + direct * here
            gated[0, pl.ds((low + b) * FLT, FLT), lanes] = (
                query[b * FLT : (b + 1) * FLT] * conv
            ).astype(jnp.bfloat16)

    @pl.loop(0, width // LANES)
    def _(tile):
        convolve(tile, 1, blocks)

    def place(owner, piece, late):
        up_y = (c // 4 + owner // 4) % 2
        up_x = (c // 2 + owner // 2) % 2
        up_core = (c + owner) % 2
        slot = (late * n_context + owner) * PIECES + piece
        block = (late * 2 + up_core) * PIECES + piece
        return slot, 2 * up_y + up_x, block

    def spot_of(block, side):
        core = block // PIECES % 2
        index = (core * 2 + side) * PIECES + block % PIECES
        return pl.ds(pl.multiple_of(index * cols, cols), cols)

    def out_copy(slot, block):
        spot = spot_of(block, half)
        lane = block % (2 * PIECES)
        return pltpu.make_async_remote_copy(
            src_ref=stage.at[slot], dst_ref=mixed.at[:, spot],
            send_sem=out_send.at[lane], recv_sem=out_recv.at[lane],
            device_id={"context": to_x}, device_id_type=MESH,
        )

    def hop_copy(slot, landing, sem, target, part):
        return pltpu.make_async_remote_copy(
            src_ref=stage.at[slot, pl.ds(*part), :], dst_ref=landing.at[pl.ds(*part), :],
            send_sem=z_send.at[slot], recv_sem=sem,
            device_id={"tensor": target}, device_id_type=MESH,
        )

    whole = (0, rows)

    def up_copy(slot, part=whole):
        return hop_copy(slot, main.at[slot], main_recv.at[slot], z + 1, part)

    def down_copy(slot, part=whole):
        return hop_copy(slot, main.at[slot], main_recv.at[slot], z - 1, part)

    def last_copy(slot, block, part=whole):
        return hop_copy(slot, extra.at[block], extra_recv.at[block], z - 1, part)

    def pass_on(slot, goal, block, part=whole):
        @pl.when(goal > z)
        def _():
            up_copy(slot, part).start()

        @pl.when(goal < z - 1)
        def _():
            down_copy(slot, part).start()

        @pl.when(goal == z - 1)
        def _():
            last_copy(slot, block, part).start()

    def depth(goal):
        last = n_tensor - 1
        return jnp.where(
            goal > z, z, jnp.where(goal < z, last - z, jnp.maximum(z, last - z))
        )

    def multiply(step, part):
        owner, piece, late, _ = arrival(step)
        slot, goal, block = place(owner, piece, late)
        stage[slot, pl.ds(*part), :] = jnp.dot(
            gated[late, pl.ds(*part), :],
            held[owner * PIECES + piece],
            preferred_element_type=jnp.float32,
        ).astype(jnp.bfloat16)

        @pl.when(depth(goal) == 0)
        def _():
            pass_on(slot, goal, block, part)

    for piece in range(PIECES):
        send_held(PIECES + piece, PIECES + piece, core_send.at[0], to_core).wait_recv()

    @pl.loop(0, EARLY)
    def _(step):
        multiply(step, (FLT, rows - FLT))

    @pl.when(c > 0)
    def _():
        halo_copies(c)[1].wait_recv()

    @pl.loop(0, width // LANES)
    def _(tile):
        convolve(tile, 0, 1)

    rows_copy = pltpu.make_async_remote_copy(
        src_ref=gated.at[0], dst_ref=gated.at[1],
        send_sem=rows_send.at[0], recv_sem=rows_recv.at[0],
        device_id={"context": to_x}, device_id_type=MESH,
    )
    rows_copy.start()

    steps = 2 * n_context * PIECES

    @pl.loop(0, steps + LAG * (n_tensor - 1))
    def _(step):
        @pl.when(step < steps)
        def _():
            owner, piece, late, fresh = arrival(step)
            slot, goal, block = place(owner, piece, late)
            chunk = owner * PIECES + piece

            @pl.when(fresh == 1)
            def _():
                send_held(chunk, chunk, core_send.at[0], to_core).wait_recv()

            @pl.when(jnp.logical_and(fresh == 1, owner % 2 == 0))
            def _():
                send_held(
                    chunk, chunk + PIECES, core_send.at[owner // 2 * PIECES + piece], to_core
                ).start()

            @pl.when(jnp.logical_and(fresh == 1, owner == 2))
            def _():
                send_held(chunk, 6 * PIECES + piece, y_send.at[PIECES + piece], to_y).start()

            for part, when in enumerate(RELAY_STEPS):
                @pl.when(step == when)
                def _(part=part):
                    send_half(part).wait_recv()
                    relay_half(part).start()
                    if part == 1:
                        send_held(
                            swapped, 3 * PIECES + 1, core_send.at[PIECES + 1], to_core
                        ).start()

            @pl.when(step == ROWS_STEP)
            def _():
                rows_copy.wait_recv()
                send_half(0).start()
                send_half(1).start()

            @pl.when(step < EARLY)
            def _():
                multiply(step, (0, FLT))

            @pl.when(step >= EARLY)
            def _():
                multiply(step, whole)

        for hop in range(1, n_tensor):
            event = step - hop * LAG
            owner, piece, late, _ = arrival(event)
            slot, goal, block = place(owner, piece, late)
            due = jnp.logical_and(
                jnp.logical_and(event >= 0, event < steps), depth(goal) == hop
            )

            @pl.when(jnp.logical_and(due, goal != z))
            def _():
                up_copy(slot).wait_recv()
                stage[slot] = (
                    stage[slot].astype(jnp.float32) + main[slot].astype(jnp.float32)
                ).astype(jnp.bfloat16)
                pass_on(slot, goal, block)

            @pl.when(jnp.logical_and(due, goal == z))
            def _():
                @pl.when(z < n_tensor - 1)
                def _():
                    last_copy(slot, block).wait_recv()

                @pl.when(z > 0)
                def _():
                    up_copy(slot).wait_recv()

                def finish(result):
                    @pl.when(late == 0)
                    def _():
                        mixed[:, spot_of(block, half)] = result

                    @pl.when(late == 1)
                    def _():
                        stage[slot] = result
                        out_copy(slot, block).start()

                @pl.when(z == 0)
                def _():
                    finish((
                        stage[slot].astype(jnp.float32) + extra[block].astype(jnp.float32)
                    ).astype(jnp.bfloat16))

                @pl.when(z == n_tensor - 1)
                def _():
                    finish((
                        stage[slot].astype(jnp.float32) + main[slot].astype(jnp.float32)
                    ).astype(jnp.bfloat16))

                @pl.when(jnp.logical_and(z > 0, z < n_tensor - 1))
                def _():
                    finish((
                        stage[slot].astype(jnp.float32)
                        + main[slot].astype(jnp.float32)
                        + extra[block].astype(jnp.float32)
                    ).astype(jnp.bfloat16))

    for lane in range(2 * PIECES):
        pltpu.make_async_remote_copy(
            src_ref=stage.at[0], dst_ref=mixed.at[:, spot_of(lane, 1 - half)],
            send_sem=out_send.at[lane], recv_sem=out_recv.at[lane],
            device_id={"context": to_x}, device_id_type=MESH,
        ).wait_recv()

    count = sites.shape[0]
    each = count // n_context
    folds = SLOTS // each
    row_at = lax.broadcasted_iota(jnp.int32, (n_context * SLOTS, 1), 0)
    local = jnp.full((n_context * SLOTS, 1), -1, jnp.int32)
    for v in range(count):
        first = v // each * SLOTS
        mine = jnp.logical_and(row_at // SLOTS * SLOTS == first, row_at % each == v % each)
        local = jnp.where(mine, sites[v] - c * rows, local)
    picks = jnp.zeros((n_context * SLOTS, outbox.shape[1]), jnp.float32)
    for fold in range(folds):
        here = jnp.where(row_at % SLOTS // each == fold, local, -1)
        one_hot = (
            lax.broadcasted_iota(jnp.int32, (n_context * SLOTS, rows), 1) == here
        ).astype(jnp.float32).astype(jnp.bfloat16)
        part = pl.ds(fold * outbox.shape[1], outbox.shape[1])
        picks = picks + jnp.dot(one_hot, mixed[:, part], preferred_element_type=jnp.float32)
    outbox[...] = picks.astype(jnp.bfloat16)

    def pick_copy(step, target):
        return pltpu.make_async_remote_copy(
            src_ref=outbox.at[pl.ds(pl.multiple_of(target * SLOTS, SLOTS), SLOTS), :],
            dst_ref=inbox.at[step - 1],
            send_sem=pick_send.at[step - 1], recv_sem=pick_recv.at[step - 1],
            device_id={"context": target}, device_id_type=MESH,
        )

    picks = [pick_copy(step, lax.rem(c + step, n_context)) for step in range(1, n_context)]
    for copy in picks:
        copy.start()
    total = outbox[pl.ds(pl.multiple_of(c * SLOTS, SLOTS), SLOTS), :].astype(jnp.float32)
    for step, copy in enumerate(picks):
        copy.wait_recv()
        total = total + inbox[step].astype(jnp.float32)
    for fold in range(folds):
        picked[:, pl.ds(fold * outbox.shape[1], outbox.shape[1])] = total[
            fold * each : (fold + 1) * each
        ].astype(jnp.bfloat16)

    for copy in picks:
        copy.wait_send()

    @pl.when(c < n_context - 1)
    def _():
        for copy in halo_copies(c + 1):
            copy.wait_send()

    rows_copy.wait_send()
    send_away(0).wait_send()
    for part in (0, 1):
        send_half(part).wait_send()
        relay_half(part).wait_send()
    for index in range(2 * PIECES):
        if index < 2 * PIECES - 1:
            send_held(0, 0, y_send.at[index], to_y).wait_send()
        out_copy(0, index).wait_send()

    @pl.loop(0, 4 * PIECES)
    def _(index):
        send_held(0, 0, core_send.at[index], to_core).wait_send()

    @pl.loop(0, steps)
    def _(step):
        owner, piece, late, _ = arrival(step)
        slot, goal, block = place(owner, piece, late)

        @pl.when(goal != z)
        def _():
            up_copy(slot).wait_send()


def fused_on_device(projected, taps, filters, skip, out_weight, positions):
    _, rows, width = projected.shape
    depth, mine = out_weight.shape
    cols = mine // (2 * PIECES)
    n_context = lax.axis_size("context")
    sites = positions.shape[0] // n_context
    groups = filters.shape[0]
    chunks = n_context * PIECES
    bf = jnp.bfloat16
    vmem = pl.BlockSpec(memory_space=pltpu.VMEM)
    hbm = pl.BlockSpec(memory_space=pl.ANY)
    dma = pltpu.SemaphoreType.DMA
    mixed, picked = pl.pallas_call(
        fused,
        out_shape=(
            jax.ShapeDtypeStruct((rows, 2 * mine), bf),
            jax.ShapeDtypeStruct((sites, 2 * mine), bf),
        ),
        in_specs=[
            hbm, vmem, vmem, vmem, hbm, pl.BlockSpec(memory_space=pltpu.SMEM)
        ],
        out_specs=(vmem, vmem),
        scratch_shapes=[
            pltpu.VMEM((3, HALO + rows, width), bf),
            pltpu.VMEM((groups, 2 * FLT), jnp.float32),
            pltpu.VMEM((groups * FLT, 2 * FLT), bf),
            pltpu.VMEM((chunks, depth, cols), bf),
            pltpu.VMEM((PIECES, depth, cols), bf),
            pltpu.VMEM((2, rows, width), bf),
            pltpu.VMEM((2 * chunks, rows, cols), bf),
            pltpu.VMEM((2 * chunks, rows, cols), bf),
            pltpu.VMEM((4 * PIECES, rows, cols), bf),
            pltpu.VMEM((n_context * SLOTS, 2 * mine * sites // SLOTS), bf),
            pltpu.VMEM((n_context - 1, SLOTS, 2 * mine * sites // SLOTS), bf),
            dma((2 * PIECES + 1,)),
            dma((2,)),
            dma((2,)),
            dma((PIECES,)),
            dma((2 * PIECES,)),
            dma((4 * PIECES,)),
            dma((chunks,)),
            dma((2 * chunks,)),
            dma((2 * chunks,)),
            dma((4 * PIECES,)),
            dma((n_context - 1,)),
            dma((n_context - 1,)),
            dma((1,)),
            dma((1,)),
            dma((2 * PIECES,)),
            dma((2 * PIECES,)),
            dma((2,)),
            dma((2,)),
            dma((2,)),
        ],
        compiler_params=pltpu.CompilerParams(
            collective_id=0, has_side_effects=True, vmem_limit_bytes=62 * 1024 * 1024
        ),
        cost_estimate=pl.CostEstimate(
            flops=2 * rows * width * mine * n_context, bytes_accessed=2**24, transcendentals=0
        ),
    )(projected, taps, filters, skip.reshape(1, width), out_weight, positions)
    return mixed, picked


def fits(mesh):
    return mesh.shape["context"] == 8 and mesh.shape["tensor"] == 4


def solution(mesh):
    return jax.shard_map(
        fused_on_device if fits(mesh) else on_device,
        mesh=mesh,
        in_specs=(
            P(None, "context", "tensor"),
            P(None, None, "tensor"),
            P("tensor", None),
            P("tensor"),
            P("tensor", "context"),
            P(),
        ),
        out_specs=(P("context", "tensor"), P("context", "tensor")),
        check_vma=False,
    )
```
